32 devices in a mesh: seq: 4 (over y, x), tm: 8 (over z, core).
Axes of the slice: x: 2, y: 2, z: 4, core: 2. Of those that a mesh axis runs over, the one named last changes fastest.
Arguments:
- tokens: bfloat16 [4, 8, 2048, 512], P(None, 'seq', 'tm'), may hold values from -6 to 6
- lengths: int32 [4, 8], P(None, 'seq'), may hold values from 256 to 2048, as said below
- cotangent: bfloat16 [4, 8, 2048, 512], P(None, 'seq', 'tm'), may hold values from -6 to 6
- norm_gain: bfloat16 [512], P(('seq', 'tm')), may hold values from 0.099609375 to 1.8984375
- norm_shift: bfloat16 [512], P(('seq', 'tm')), may hold values from -3 to 3
- input_proj: bfloat16 [512, 512], P(('seq', 'tm')), may hold values from -0.25 to 0.25
- decay_log: bfloat16 [256], P(('seq', 'tm')), may hold values from -13 to 0
- phase_log: bfloat16 [256], P(('seq', 'tm')), may hold values from -5 to -0.5
- gamma_log: bfloat16 [256], P(('seq', 'tm')), may hold values from -7 to 1
- output_proj: bfloat16 [512, 512], P(('seq', 'tm')), may hold values from -0.25 to 0.25
- skip_gain: bfloat16 [512], P(('seq', 'tm')), may hold values from -3 to 3
- gate_weight: bfloat16 [512, 1024], P(('seq', 'tm')), may hold values from -0.75 to 0.75
- gate_bias: bfloat16 [1024], P(('seq', 'tm')), may hold values from -3 to 3
Outputs:
- block_out: bfloat16 [4, 8, 2048, 512], P(None, 'seq', 'tm')
- tokens_gradient: bfloat16 [4, 8, 2048, 512], P(None, 'seq', 'tm')
- norm_gain_gradient: float32 [512], P(('seq', 'tm'))
- norm_shift_gradient: float32 [512], P(('seq', 'tm'))
- input_proj_gradient: float32 [512, 512], P(('seq', 'tm'))
- decay_log_gradient: float32 [256], P(('seq', 'tm'))
- phase_log_gradient: float32 [256], P(('seq', 'tm'))
- gamma_log_gradient: float32 [256], P(('seq', 'tm'))
- output_proj_gradient: float32 [512, 512], P(('seq', 'tm'))
- skip_gain_gradient: float32 [512], P(('seq', 'tm'))
- gate_weight_gradient: float32 [512, 1024], P(('seq', 'tm'))
- gate_bias_gradient: float32 [1024], P(('seq', 'tm'))
The draws below stay inside these ranges and needn't reach their ends.
Inputs may be any that keep to these rules, and one draw needn't show every extreme that they name: `lengths`: in every micro-batch, among the 2 sequences that share an index of seq, one uses all 2048 positions; positions from a sequence's length on are padding.
All inputs are finite; a program needn't handle non-finite values.
Results may differ from the reference program's by a relative error of at most 0.02.
Values may be sent and summed in bfloat16 or wider, within the bound.
No kernel may reach another device: no remote copies, remote signals or barrier semaphores. Data moves between devices by JAX's collectives and lax.ppermute only.
A program may use at most 128 MiB of HBM per device.

```python
import jax
import jax.numpy as jnp
from jax import lax

WIDTH = 512
STATE = 256
SEQ_DEV = 2
MICRO = 4
LENGTH = 2048
SEQ_ALL = 8


def decay_rates(key, fast_share):
    chooser = jax.random.uniform(jax.random.fold_in(key, 101), (STATE,))
    slow_log = jax.random.uniform(jax.random.fold_in(key, 102), (STATE,), minval=jnp.log(0.3 / LENGTH), maxval=jnp.log(2.0 / LENGTH))
    fast_log = jax.random.uniform(jax.random.fold_in(key, 103), (STATE,), minval=jnp.log(1.0 / 50.0), maxval=jnp.log(1.0 / 30.0))
    return jnp.exp(jnp.where(chooser < fast_share, fast_log, slow_log))


def draw_decay_log(key, part):
    rates = decay_rates(key, 0.5)
    return jnp.log(rates).astype(jnp.bfloat16)


def draw_gamma_log(key, part):
    rates = decay_rates(key, 0.5)
    key = jax.random.fold_in(key, 8)
    jitter = jax.random.uniform(key, (STATE,), minval=-0.3, maxval=0.3)
    return (0.5 * jnp.log1p(-jnp.exp(-2.0 * rates)) + jitter).astype(jnp.bfloat16)


def draw_lengths(key, part):
    key = jax.random.fold_in(key, 9)
    groups = SEQ_ALL // SEQ_DEV
    full_slot = jax.random.randint(jax.random.fold_in(key, 1), (MICRO, groups, 1), 0, SEQ_DEV)
    drawn = jax.random.randint(jax.random.fold_in(key, 2), (MICRO, groups, SEQ_DEV), LENGTH // 8, LENGTH + 1)
    slots = jnp.arange(SEQ_DEV, dtype=jnp.int32)
    whole = jnp.where(slots == full_slot, LENGTH, drawn)
    return whole.reshape(MICRO, SEQ_ALL).astype(jnp.int32)


def level_of(own_key, dims, cuts, low, top_value):
    factor_of, own = 1.0, jax.random.fold_in(own_key, 6)
    for dim, parts in cuts:
        heights = jnp.exp(jax.random.uniform(jax.random.fold_in(own, dim), (parts,), jnp.float32, low / len(cuts), top_value / len(cuts)))
        factor_of = factor_of * jnp.repeat(heights, dims[dim] // parts).reshape([-1 if axis == dim else 1 for axis in range(len(dims))])
    return factor_of


def gaussian(key, extent, spread, most, pieces=(), held_as=jnp.bfloat16):
    level = level_of(key, extent, pieces, -0.22, 0.18) if pieces else 1.0
    entries = jax.random.normal(key, extent, jnp.float32) * spread * level
    return jnp.minimum(jnp.maximum(entries, -most), most).astype(held_as)


def setup_inputs(seed: int = 0) -> dict:
    key_of = jax.random.split(jax.random.key(seed), 14)
    return {
        "tokens": gaussian(key_of[0], (MICRO, SEQ_ALL, LENGTH, WIDTH), 1.0, 6.0, ((1, 4), (2, 8))),
        "lengths": draw_lengths(jax.random.fold_in(key_of[13], 71), 0),
        "cotangent": gaussian(key_of[2], (MICRO, SEQ_ALL, LENGTH, WIDTH), 1.0, 6.0, ((1, 4), (2, 8))),
        "norm_gain": jnp.clip(1.0 + 0.18 * jax.random.normal(key_of[3], (WIDTH,), jnp.float32), 0.099609375, 1.8984375).astype(jnp.bfloat16),
        "norm_shift": gaussian(key_of[4], (WIDTH,), 0.5, 3.0, ((0, 32),)),
        "input_proj": gaussian(key_of[5], (WIDTH, 2 * STATE), WIDTH ** -0.5, 0.25, ((0, 32),)),
        "decay_log": draw_decay_log(jax.random.fold_in(key_of[13], 71), 0),
        "phase_log": jnp.clip(-5.0 + 4.5 * jax.random.uniform(key_of[7], (STATE,), jnp.float32) ** level_of(key_of[7], (STATE,), ((0, 32),), -0.2, 0.2), -5.0, -0.5).astype(jnp.bfloat16),
        "gamma_log": draw_gamma_log(jax.random.fold_in(key_of[13], 71), 0),
        "output_proj": gaussian(key_of[9], (2 * STATE, WIDTH), (2 * STATE) ** -0.5, 0.25, ((0, 32),)),
        "skip_gain": gaussian(key_of[10], (WIDTH,), 0.5, 3.0, ((0, 32),)),
        "gate_weight": gaussian(key_of[11], (WIDTH, 2 * WIDTH), (WIDTH // 8) ** -0.5, 0.75, ((0, 32),)),
        "gate_bias": gaussian(key_of[12], (2 * WIDTH,), 0.5, 3.0, ((0, 32),)),
    }


@jax.custom_vjp
def low(v):
    return lax.optimization_barrier(v.astype(jnp.bfloat16)).astype(jnp.float32)

@jax.custom_vjp
def low_back(v):
    return v

def low_keep(v):
    return (low(v), None)

def low_pass(kept, grad):
    return (grad,)

def back_keep(v):
    return (v, None)

def back_low(kept, grad):
    return (low(grad),)
low.defvjp(low_keep, low_pass)
low_back.defvjp(back_keep, back_low)

def pair_combine(earlier, latter):
    early_mul_re, early_mul_im, early_add_re, early_add_im = earlier
    late_mul_re, late_mul_im, late_add_re, late_add_im = latter
    return (late_mul_re * early_mul_re - late_mul_im * early_mul_im, late_mul_re * early_mul_im + late_mul_im * early_mul_re, late_mul_re * early_add_re - late_mul_im * early_add_im + late_add_re, late_mul_re * early_add_im + late_mul_im * early_add_re + late_add_im)

def recurrence(lam_re, lam_im, drive_re, drive_im):
    factor_re = jnp.broadcast_to(lam_re, drive_re.shape)
    factor_im = jnp.broadcast_to(lam_im, drive_im.shape)
    scanned = lax.associative_scan(pair_combine, (factor_re, factor_im, drive_re, drive_im), axis=0)
    return (scanned[2], scanned[3])

def product(left_side, right_side):
    return jnp.dot(left_side, right_side, precision=lax.Precision.HIGHEST, preferred_element_type=jnp.float32)

def residual_block(params, inputs, live_mask):
    norm_gain, norm_shift, input_proj, decay_log, phase_log, gamma_log, output_proj, skip_gain, gate_weight, gate_bias = params
    average = lax.optimization_barrier(jnp.mean(inputs, axis=-1, keepdims=True))
    centred = inputs - average
    variance = lax.optimization_barrier(jnp.mean(centred * centred, axis=-1, keepdims=True))
    normed = low(centred * lax.rsqrt(variance + 1e-05) * norm_gain + norm_shift)
    drive = low_back(product(normed, input_proj))
    state_count = decay_log.shape[0]
    decay_rate = jnp.exp(decay_log)
    phase_step = jnp.exp(phase_log)
    modulus = jnp.exp(-decay_rate)
    lam_re = modulus * jnp.cos(phase_step)
    lam_im = modulus * jnp.sin(phase_step)
    input_scale = jnp.exp(gamma_log)
    state_re, state_im = recurrence(lam_re, lam_im, input_scale * drive[:, :state_count], input_scale * drive[:, state_count:])
    state_low = low(jnp.concatenate([state_re, state_im], axis=-1))
    mixed = low_back(product(state_low, output_proj) + skip_gain * normed)
    activated = low(jax.nn.gelu(mixed))
    gated = low_back(product(activated, gate_weight) + gate_bias)
    model_width = inputs.shape[-1]
    return inputs + live_mask[:, None] * gated[:, :model_width] * jax.nn.sigmoid(gated[:, model_width:])

def reference(tokens, lengths, cotangent, norm_gain, norm_shift, input_proj, decay_log, phase_log, gamma_log, output_proj, skip_gain, gate_weight, gate_bias):
    params = tuple((weight.astype(jnp.float32) for weight in (norm_gain, norm_shift, input_proj, decay_log, phase_log, gamma_log, output_proj, skip_gain, gate_weight, gate_bias)))
    seq_total = tokens.shape[0] * tokens.shape[1]
    seq_len = tokens.shape[2]
    model_width = tokens.shape[3]
    flat_tokens = tokens.reshape(seq_total, seq_len, model_width)
    flat_cotangent = cotangent.reshape(seq_total, seq_len, model_width)
    flat_lengths = lengths.reshape(seq_total).astype(jnp.int32)
    positions = jnp.arange(seq_len, dtype=jnp.int32)

    def one_sequence(totals, sequence_item):
        sequence, length, incoming = sequence_item
        live_mask = (positions < length).astype(jnp.float32)

        def forward(weights, inputs):
            return residual_block(weights, inputs, live_mask)
        result, pullback = jax.vjp(forward, params, sequence.astype(jnp.float32))
        weight_grads, input_grad = pullback(incoming.astype(jnp.float32))
        totals = jax.tree.map(jnp.add, totals, weight_grads)
        return (totals, (result.astype(jnp.bfloat16), input_grad.astype(jnp.bfloat16)))
    zero_grads = tuple((jnp.zeros(weight.shape, jnp.float32) for weight in params))
    totals, (outputs, input_grads) = lax.scan(one_sequence, zero_grads, (flat_tokens, flat_lengths, flat_cotangent))
    return (outputs.reshape(tokens.shape), input_grads.reshape(tokens.shape), totals[0], totals[1], totals[2], totals[3], totals[4], totals[5], totals[6], totals[7], totals[8], totals[9])
```

```python
import math

import jax
import jax.numpy as jnp
from jax import lax
from jax.experimental import pallas as pl
from jax.experimental.pallas import tpu as pltpu
from jax.sharding import Mesh, PartitionSpec as P

F32 = jnp.float32
BF = jnp.bfloat16
AXES = ("seq", "tmc", "core")
CHIPS = ("seq", "tmc")
LIMIT = pltpu.CompilerParams(vmem_limit_bytes=56 << 20)
GELU_K = math.sqrt(2.0 / math.pi)
STEPS = 32


def dot(a, b):
    return lax.dot_general(a, b, (((1,), (0,)), ((), ())), preferred_element_type=F32)


def dot_rows(a, b):
    return lax.dot_general(a, b, (((0,), (0,)), ((), ())), preferred_element_type=F32)


def whole(shape):
    return pl.BlockSpec(shape, lambda *_: (0,) * len(shape))


def prepare_kernel(span, base, tok, cot, wh_out, wht_out, inv_out, cotl_out):
    count, length, width = tok.shape
    part = 16
    for i in range(0, length, part):
        x = tok[:, i : i + part, :].astype(F32)
        mean = jnp.mean(x, axis=-1, keepdims=True)
        c = x - mean
        inv = lax.rsqrt(jnp.mean(c * c, axis=-1, keepdims=True) + 1e-05)
        wh = jnp.swapaxes(c * inv, 0, 1).reshape(part * count, width)
        rows = slice(i * count, (i + part) * count)
        wh_out[rows, :] = wh.astype(BF)
        wide = jnp.broadcast_to(inv, (count, part, 128))
        inv_out[rows, :] = jnp.swapaxes(wide, 0, 1).reshape(part * count, 128)
        y = jnp.swapaxes(cot[:, i : i + part, :].astype(F32), 0, 1)
        seq_id = lax.broadcasted_iota(jnp.int32, (1, count, 128), 1)
        ends = jnp.zeros((1, count, 128), jnp.int32)
        for s in range(count):
            ends = jnp.where(seq_id == s, span[s], ends)
        place = base[0] + i + lax.broadcasted_iota(jnp.int32, (part, 1, 128), 0)
        live = jnp.where(place < ends, 1.0, 0.0)
        y = y * jnp.concatenate([live] * (width // 128), axis=-1)
        cotl_out[rows, :] = y.reshape(part * count, width).astype(BF)
    step = 256
    for i in range(0, length * count, step):
        wht_out[:, i : i + step] = wh_out[i : i + step, :].T


def prepare(span, base, tok, cot):
    count, length, width = tok.shape
    total = count * length
    smem = pl.BlockSpec(memory_space=pltpu.SMEM)
    return pl.pallas_call(
        prepare_kernel,
        out_shape=(
            jax.ShapeDtypeStruct((total, width), BF),
            jax.ShapeDtypeStruct((width, total), BF),
            jax.ShapeDtypeStruct((total, 128), F32),
            jax.ShapeDtypeStruct((total, width), BF),
        ),
        in_specs=[smem, smem, whole(tok.shape), whole(cot.shape)],
        compiler_params=LIMIT,
        name="prepare",
    )(span, base, tok, cot)


def assemble_one(place, dests, own, other):
    pieces = own.shape[0]
    for half, ref in enumerate((own, other)):
        for q in range(pieces):
            owner = jnp.bitwise_xor(place, 2 * q + half)
            row = pl.multiple_of(owner * 16, 16)
            for k, d in enumerate(dests):
                d[pl.ds(row, 16), :] = ref[q, 16 * k : 16 * (k + 1), :]


def vector_rows(acc):
    half = acc.shape[1] // 2
    gain, shift, skip = acc[0:1], acc[1:2], acc[2:3]
    rate = jnp.exp(acc[3:4, :half])
    phase = jnp.exp(acc[3:4, half:])
    scale = jnp.exp(acc[4:5])
    modulus = jnp.exp(-rate)
    lam = jnp.concatenate([modulus * jnp.cos(phase), modulus * jnp.sin(phase)], axis=1)
    rates = jnp.concatenate([rate, phase], axis=1)
    shifted = (acc[7:8] + acc[8:9]) * scale
    return (lam, rates, scale, shifted, skip * gain, skip * shift, acc[5:6], acc[6:7])


def assemble_first_kernel(place, own, other, b_out, bt_out, vec_out):
    pieces, _, width = own.shape
    acc = jnp.zeros((16, width), F32)
    for ref in (own, other):
        for q in range(pieces):
            acc = acc + ref[q, 16:32, :].astype(F32)
    rows = vector_rows(acc)
    for k, r in enumerate(rows):
        vec_out[k : k + 1, :] = r
    assemble_one(place[0], (b_out,), own, other)
    b_out[...] = (b_out[...].astype(F32) * rows[2]).astype(BF)
    bt_out[...] = b_out[...].T


def assemble_first(place, own, other):
    width = own.shape[-1]
    smem = pl.BlockSpec(memory_space=pltpu.SMEM)
    return pl.pallas_call(
        assemble_first_kernel,
        out_shape=(
            jax.ShapeDtypeStruct((width, width), BF),
            jax.ShapeDtypeStruct((width, width), BF),
            jax.ShapeDtypeStruct((8, width), F32),
        ),
        in_specs=[smem, whole(own.shape), whole(other.shape)],
        compiler_params=LIMIT,
        name="assemble_first",
    )(place, own, other)


def assemble_rest_kernel(place, own, other, c_out, ct_out, g_out, gt_out):
    width = c_out.shape[0]
    assemble_one(place[0], (c_out, g_out.at[:, :width], g_out.at[:, width:]), own, other)
    ct_out[...] = c_out[...].T
    gt_out[...] = g_out[...].T


def assemble_rest(place, own, other):
    width = own.shape[-1]
    smem = pl.BlockSpec(memory_space=pltpu.SMEM)
    return pl.pallas_call(
        assemble_rest_kernel,
        out_shape=(
            jax.ShapeDtypeStruct((width, width), BF),
            jax.ShapeDtypeStruct((width, width), BF),
            jax.ShapeDtypeStruct((width, 2 * width), BF),
            jax.ShapeDtypeStruct((2 * width, width), BF),
        ),
        in_specs=[smem, whole(own.shape), whole(other.shape)],
        compiler_params=LIMIT,
        name="assemble_rest",
    )(place, own, other)


def complex_step(lr, li, xr, xi, ur, ui):
    return lr * xr - li * xi + ur, lr * xi + li * xr + ui


def lam_rows(vec, count):
    half = vec.shape[1] // 2
    return (
        jnp.broadcast_to(vec[0:1, :half], (count, half)),
        jnp.broadcast_to(vec[0:1, half:], (count, half)),
    )


def drive_kernel(wh, b, vec, u_out, end_out):
    i = pl.program_id(0)
    count, width = end_out.shape
    half = width // 2

    @pl.when(i == 0)
    def _():
        end_out[...] = jnp.zeros_like(end_out)

    u_out[...] = dot(wh[...], b[...]) + vec[3:4, :]
    lr, li = lam_rows(vec, count)
    xr, xi = end_out[:, :half], end_out[:, half:]
    for t in range(u_out.shape[0] // count):
        rows = slice(t * count, (t + 1) * count)
        xr, xi = complex_step(lr, li, xr, xi, u_out[rows, :half], u_out[rows, half:])
    end_out[:, :half] = xr
    end_out[:, half:] = xi


def drive(wh, b, vec, count):
    total, width = wh.shape
    rows = STEPS * count
    return pl.pallas_call(
        drive_kernel,
        grid=(total // rows,),
        out_shape=(
            jax.ShapeDtypeStruct((total, width), F32),
            jax.ShapeDtypeStruct((count, width), F32),
        ),
        in_specs=[
            pl.BlockSpec((rows, width), lambda i: (i, 0)),
            whole(b.shape),
            whole(vec.shape),
        ],
        out_specs=(
            pl.BlockSpec((rows, width), lambda i: (i, 0)),
            whole((count, width)),
        ),
        compiler_params=LIMIT,
        name="drive",
    )(wh, b, vec)


def middle_kernel(
    span, base, u, wh, cotl, tok, carry, vec, c, ct, g, gt,
    block_out, st_out, act_out, dpre_out, dm_out, dst_out, end_out, sums_out, bias_out,
    state, sbuf, mix, pre, slope, dact, power,
):
    i = pl.program_id(0)
    count, width = end_out.shape
    half = width // 2
    rows = u.shape[0]
    steps = rows // count

    @pl.when(i == 0)
    def _():
        state[...] = carry[...]
        end_out[...] = jnp.zeros_like(end_out)
        sums_out[...] = jnp.zeros_like(sums_out)
        bias_out[...] = jnp.zeros_like(bias_out)
        power[:, :half] = jnp.ones((count, half), F32)
        power[:, half:] = jnp.zeros((count, half), F32)

    lr, li = lam_rows(vec, count)
    xr, xi = state[:, :half], state[:, half:]
    for t in range(steps):
        r = slice(t * count, (t + 1) * count)
        xr, xi = complex_step(lr, li, xr, xi, u[r, :half], u[r, half:])
        sbuf[r, :half] = xr
        sbuf[r, half:] = xi
    state[:, :half] = xr
    state[:, half:] = xi
    st_out[...] = sbuf[...].astype(BF)
    mix[...] = dot(st_out[...], c[...])
    part = 32
    for k in range(0, rows, part):
        r = slice(k, k + part)
        x = mix[r, :] + wh[r, :].astype(F32) * vec[4:5, :] + vec[5:6, :]
        sq = x * x
        th = jnp.tanh(x * (GELU_K + (GELU_K * 0.044715) * sq))
        q = 0.5 * th + 0.5
        a = x * q
        act_out[r, :] = a.astype(BF)
        slope[r, :] = q + a * (1.0 - q) * (2.0 * GELU_K + (6.0 * GELU_K * 0.044715) * sq)
    pre[...] = dot(act_out[...], g[...])
    seq_id = lax.broadcasted_iota(jnp.int32, (count, 128), 0)
    ends = jnp.zeros((count, 128), jnp.int32)
    for s in range(count):
        ends = jnp.where(seq_id == s, span[s], ends)
    first = base[0] + i * steps
    bias_v = jnp.zeros((count, width), F32)
    bias_g = jnp.zeros((count, width), F32)
    for k in range(0, rows, part):
        r = slice(k, k + part)
        v = pre[r, :width] + vec[6:7, :]
        gate = pre[r, width:] + vec[7:8, :]
        sig = 0.5 * jnp.tanh(0.5 * gate) + 0.5
        y = v * sig
        ct_live = cotl[r, :].astype(F32)
        dv = ct_live * sig
        dg = ct_live * y * (1.0 - sig)
        dpre_out[r, :width] = dv.astype(BF)
        dpre_out[r, width:] = dg.astype(BF)
        n = part // count
        bias_v = bias_v + jnp.sum(dv.reshape(n, count, width), axis=0)
        bias_g = bias_g + jnp.sum(dg.reshape(n, count, width), axis=0)
        t0 = k // count
        place = first + t0 + lax.broadcasted_iota(jnp.int32, (n, 1, 128), 0)
        live = jnp.where(place < ends[None], 1.0, 0.0)
        y = y.reshape(n, count, width) * jnp.concatenate([live] * (width // 128), axis=-1)
        mix[r, :] = y.reshape(part, width)
    bias_out[:, :width] += bias_v
    bias_out[:, width:] += bias_g
    for k in range(0, steps, 16):
        y = jnp.swapaxes(mix[k * count : (k + 16) * count, :].reshape(16, count, width), 0, 1)
        block_out[:, k : k + 16, :] = (tok[:, k : k + 16, :].astype(F32) + y).astype(BF)
    dact[...] = dot(dpre_out[...], gt[...])
    s1 = jnp.zeros((count, width), F32)
    s2 = jnp.zeros((count, width), F32)
    for k in range(0, rows, part):
        r = slice(k, k + part)
        d = dact[r, :] * slope[r, :]
        dm_out[r, :] = d.astype(BF)
        n = part // count
        s1 = s1 + jnp.sum((d * wh[r, :].astype(F32)).reshape(n, count, width), axis=0)
        s2 = s2 + jnp.sum(d.reshape(n, count, width), axis=0)
    sums_out[:, :width] += s1
    sums_out[:, width:] += s2
    dst_out[...] = dot(dm_out[...], ct[...])
    ar = jnp.zeros((count, half), F32)
    ai = jnp.zeros((count, half), F32)
    for t in range(steps - 1, -1, -1):
        r = slice(t * count, (t + 1) * count)
        ar, ai = complex_step(lr, -li, ar, ai, dst_out[r, :half], dst_out[r, half:])
    pr, pi = power[:, :half], power[:, half:]
    end_out[:, :half] += pr * ar - pi * ai
    end_out[:, half:] += pr * ai + pi * ar
    br, bi = lr, -li
    for _ in range(int(math.log2(steps))):
        br, bi = br * br - bi * bi, 2.0 * br * bi
    power[:, :half] = pr * br - pi * bi
    power[:, half:] = pr * bi + pi * br


def middle(span, base, u, wh, cotl, tok, carry, vec, c, ct, g, gt):
    total, width = u.shape
    count = carry.shape[0]
    length = total // count
    rows = STEPS * count
    smem = pl.BlockSpec(memory_space=pltpu.SMEM)

    def block(w):
        return pl.BlockSpec((rows, w), lambda i: (i, 0))

    side = pl.BlockSpec((count, STEPS, width), lambda i: (0, i, 0))
    return pl.pallas_call(
        middle_kernel,
        grid=(total // rows,),
        out_shape=(
            jax.ShapeDtypeStruct((count, length, width), BF),
            jax.ShapeDtypeStruct((total, width), BF),
            jax.ShapeDtypeStruct((total, width), BF),
            jax.ShapeDtypeStruct((total, 2 * width), BF),
            jax.ShapeDtypeStruct((total, width), BF),
            jax.ShapeDtypeStruct((total, width), F32),
            jax.ShapeDtypeStruct((count, width), F32),
            jax.ShapeDtypeStruct((count, 2 * width), F32),
            jax.ShapeDtypeStruct((count, 2 * width), F32),
        ),
        in_specs=[
            smem, smem, block(width), block(width), block(width), side, whole(carry.shape),
            whole(vec.shape), whole(c.shape), whole(ct.shape), whole(g.shape), whole(gt.shape),
        ],
        out_specs=(
            side, block(width), block(width), block(2 * width), block(width), block(width),
            whole((count, width)), whole((count, 2 * width)), whole((count, 2 * width)),
        ),
        scratch_shapes=[
            pltpu.VMEM((count, width), F32),
            pltpu.VMEM((rows, width), F32),
            pltpu.VMEM((rows, width), F32),
            pltpu.VMEM((rows, 2 * width), F32),
            pltpu.VMEM((rows, width), F32),
            pltpu.VMEM((rows, width), F32),
            pltpu.VMEM((count, width), F32),
        ],
        compiler_params=LIMIT,
        name="middle",
    )(span, base, u, wh, cotl, tok, carry, vec, c, ct, g, gt)


def weights_kernel(st, act, dpre, dm, gate_out, proj_out, acc_gate, acc_proj):
    i = pl.program_id(0)

    @pl.when(i == 0)
    def _():
        acc_gate[...] = jnp.zeros_like(acc_gate)
        acc_proj[...] = jnp.zeros_like(acc_proj)

    acc_gate[...] += dot_rows(act[...], dpre[...])
    acc_proj[...] += dot_rows(st[...], dm[...])

    @pl.when(i == pl.num_programs(0) - 1)
    def _():
        gate_out[...] = acc_gate[...].astype(BF)
        proj_out[...] = acc_proj[...].astype(BF)


def weights(st, act, dpre, dm):
    total, width = st.shape
    rows = 512

    def block(w):
        return pl.BlockSpec((rows, w), lambda i: (i, 0))

    return pl.pallas_call(
        weights_kernel,
        grid=(total // rows,),
        out_shape=(
            jax.ShapeDtypeStruct((width, 2 * width), BF),
            jax.ShapeDtypeStruct((width, width), BF),
        ),
        in_specs=[block(width), block(width), block(2 * width), block(width)],
        out_specs=(whole((width, 2 * width)), whole((width, width))),
        scratch_shapes=[pltpu.VMEM((width, 2 * width), F32), pltpu.VMEM((width, width), F32)],
        compiler_params=LIMIT,
        name="weights",
    )(st, act, dpre, dm)


def adjoint_kernel(dst, u, st, wht, back, carry, vec, adj_out, m_out, sums_out, now, acc):
    i = pl.program_id(0)
    count, width = back.shape
    half = width // 2
    rows = dst.shape[0]
    steps = rows // count

    @pl.when(i == 0)
    def _():
        now[...] = back[...]
        sums_out[...] = jnp.zeros_like(sums_out)
        acc[...] = jnp.zeros_like(acc)

    lr, li = lam_rows(vec, count)
    ar, ai = now[:, :half], now[:, half:]
    zero = jnp.zeros((count, half), F32)
    lsr, lsi, gam, csr, csi = zero, zero, zero, zero, zero
    for t in range(steps - 1, -1, -2):
        pair = slice((t - 1) * count, (t + 1) * count)
        both = st[pair, :].astype(F32)
        held = []
        for k in (1, 0):
            r = slice((t - 1 + k) * count, (t + k) * count)
            s = both[k * count : (k + 1) * count, :]
            sr, si = s[:, :half], s[:, half:]
            mr, mi = ar, ai
            if t == steps - 1 and k == 1:
                mr, mi = jnp.where(i == 0, 0.0, ar), jnp.where(i == 0, 0.0, ai)
            lsr = lsr + mr * sr + mi * si
            lsi = lsi + mi * sr - mr * si
            ar, ai = complex_step(lr, -li, ar, ai, dst[r, :half], dst[r, half:])
            gam = gam + ar * u[r, :half] + ai * u[r, half:]
            csr = csr + ar
            csi = csi + ai
            held.append(jnp.concatenate([ar, ai], axis=1))
        adj_out[pair, :] = jnp.concatenate([held[1], held[0]], axis=0).astype(BF)
    now[:, :half] = ar
    now[:, half:] = ai
    sums_out[0:count, :half] += lsr
    sums_out[0:count, half:] += lsi
    sums_out[count : 2 * count, :half] += csr
    sums_out[count : 2 * count, half:] += csi
    sums_out[2 * count :, :half] += gam
    acc[...] += dot(wht[...], adj_out[...])

    @pl.when(i == pl.num_programs(0) - 1)
    def _():
        cr, ci = carry[:, :half], carry[:, half:]
        sums_out[0:count, :half] += ar * cr + ai * ci
        sums_out[0:count, half:] += ai * cr - ar * ci
        m_out[...] = acc[...].astype(BF)


def adjoint(dst, u, st, wht, back, carry, vec):
    total, width = u.shape
    count = carry.shape[0]
    rows = STEPS * count
    blocks = total // rows

    def block(w):
        return pl.BlockSpec((rows, w), lambda i: (blocks - 1 - i, 0))

    return pl.pallas_call(
        adjoint_kernel,
        grid=(blocks,),
        out_shape=(
            jax.ShapeDtypeStruct((total, width), BF),
            jax.ShapeDtypeStruct((width, width), BF),
            jax.ShapeDtypeStruct((3 * count, width), F32),
        ),
        in_specs=[
            block(width), block(width), block(width),
            pl.BlockSpec((width, rows), lambda i: (0, blocks - 1 - i)),
            whole(back.shape), whole(carry.shape), whole(vec.shape),
        ],
        out_specs=(block(width), whole((width, width)), whole((3 * count, width))),
        scratch_shapes=[pltpu.VMEM((count, width), F32), pltpu.VMEM((width, width), F32)],
        compiler_params=LIMIT,
        name="adjoint",
    )(dst, u, st, wht, back, carry, vec)


def inputs_kernel(adj, dm, wh, inv, cot, bt, vec, grad_out, buf):
    count, steps, width = cot.shape
    buf[...] = dot(adj[...], bt[...])
    for k in range(0, steps, 16):
        r = slice(k * count, (k + 16) * count)
        w = wh[r, :].astype(F32)
        e = buf[r, :] + dm[r, :].astype(F32) * vec[4:5, :]
        mean = jnp.mean(e, axis=-1, keepdims=True)
        proj = jnp.mean(e * w, axis=-1, keepdims=True)
        wide = jnp.concatenate([inv[r, :]] * (width // 128), axis=-1)
        d = (e - mean - w * proj) * wide
        d = jnp.swapaxes(d.reshape(16, count, width), 0, 1)
        grad_out[:, k : k + 16, :] = (cot[:, k : k + 16, :].astype(F32) + d).astype(BF)


def inputs_gradient(adj, dm, wh, inv, cot, bt, vec):
    total, width = adj.shape
    count, length, _ = cot.shape
    rows = STEPS * count

    def block(w):
        return pl.BlockSpec((rows, w), lambda i: (i, 0))

    side = pl.BlockSpec((count, STEPS, width), lambda i: (0, i, 0))
    return pl.pallas_call(
        inputs_kernel,
        grid=(total // rows,),
        out_shape=jax.ShapeDtypeStruct(cot.shape, BF),
        in_specs=[
            block(width), block(width), block(width), block(128), side,
            whole(bt.shape), whole(vec.shape),
        ],
        out_specs=side,
        scratch_shapes=[pltpu.VMEM((rows, width), F32)],
        compiler_params=LIMIT,
        name="inputs_gradient",
    )(adj, dm, wh, inv, cot, bt, vec)


def swap(a, axis, size, bit):
    return lax.ppermute(a, axis, [(k, k ^ bit) for k in range(size)])


def spread(a, axis, size):
    parts = [a] + [swap(a, axis, size, k) for k in range(1, size)]
    return jnp.stack(parts)


def complex_mul(ar, ai, br, bi):
    return ar * br - ai * bi, ar * bi + ai * br


def carry_in(end, rates, length, place, axes_sizes, backward):
    half = end.shape[1] // 2
    rate, phase = rates[:half], rates[half:]
    sign = -1.0 if backward else 1.0

    def power(steps):
        steps = jnp.asarray(steps * length, F32)
        size = jnp.exp(-steps * rate)
        return size * jnp.cos(steps * phase), sign * size * jnp.sin(steps * phase)

    total_re, total_im = end[:, :half], end[:, half:]
    pre_re = jnp.zeros_like(total_re)
    pre_im = jnp.zeros_like(total_im)
    width = 1
    tm_size = axes_sizes["tmc"] * axes_sizes["core"]
    offset = place if not backward else tm_size - 1 - place
    while width < tm_size:
        both = jnp.concatenate([total_re, total_im], axis=1)
        if width == 1:
            got = swap(both, "core", 2, 1)
        else:
            got = swap(both, "tmc", axes_sizes["tmc"], width // 2)
        got_re, got_im = got[:, :half], got[:, half:]
        later = (offset // width) % 2 == 1
        ahead = offset % width
        mul_re, mul_im = power(ahead)
        add_re, add_im = complex_mul(mul_re, mul_im, got_re, got_im)
        pre_re = pre_re + jnp.where(later, add_re, 0.0)
        pre_im = pre_im + jnp.where(later, add_im, 0.0)
        wide_re, wide_im = power(width)
        first_re = jnp.where(later, got_re, total_re)
        first_im = jnp.where(later, got_im, total_im)
        last_re = jnp.where(later, total_re, got_re)
        last_im = jnp.where(later, total_im, got_im)
        move_re, move_im = complex_mul(wide_re, wide_im, first_re, first_im)
        total_re, total_im = last_re + move_re, last_im + move_im
        width *= 2
    return jnp.concatenate([pre_re, pre_im], axis=1)


def two_rows(row):
    high = row.astype(BF)
    return high, (row - high.astype(F32)).astype(BF)


def by_owner(row, owners):
    return row.reshape(owners, -1)


def reduce_to_owner(pack, core, chips):
    owners, rows, width = pack.shape
    halves = pack.reshape(chips, 2, rows, width)
    keep = lax.dynamic_index_in_dim(halves, core, 1, False)
    give = lax.dynamic_index_in_dim(halves, 1 - core, 1, False)
    got = swap(give, "core", 2, 1)
    both = (keep.astype(F32) + got.astype(F32)).astype(BF)
    parts = lax.all_to_all(both, CHIPS, 0, 0)
    return jnp.sum(parts.astype(F32), axis=0)


def make_body(sizes):
    chips = sizes["seq"] * sizes["tmc"]
    owners = chips * 2

    def body(
        tokens, lengths, cotangent, norm_gain, norm_shift, input_proj, decay_log, phase_log,
        gamma_log, output_proj, skip_gain, gate_weight, gate_bias,
    ):
        micro, per, length, width = tokens.shape
        count = micro * per
        half = width // 2
        core = lax.axis_index("core")
        chip_tm = lax.axis_index("tmc")
        tm_place = chip_tm * 2 + core
        place = lax.axis_index("seq") * (2 * sizes["tmc"]) + tm_place
        place_s = place.astype(jnp.int32).reshape(1)
        base = (tm_place * length).astype(jnp.int32).reshape(1)
        span = lengths.reshape(count)
        tok = tokens.reshape(count, length, width)
        cot = cotangent.reshape(count, length, width)

        gain = norm_gain.astype(F32)
        shift = norm_shift.astype(F32)
        skip = skip_gain.astype(F32)
        proj = input_proj.astype(F32)

        def placed(v):
            n = v.shape[0]
            wide = jnp.broadcast_to(v[None], (owners, n))
            mine = lax.broadcasted_iota(jnp.int32, (owners, n), 0) == place
            return jnp.where(mine, wide, jnp.zeros_like(wide)).reshape(owners * n)

        bias_row = placed(gate_bias)
        shifted = jnp.sum(shift[:, None] * proj, axis=0)
        shift_hi, shift_lo = two_rows(shifted)
        vec_rows = [
            placed(norm_gain), placed(norm_shift), placed(skip_gain),
            jnp.concatenate([placed(decay_log), placed(phase_log)]),
            jnp.concatenate([placed(gamma_log), placed(gamma_log)]),
            bias_row[:width], bias_row[width:], shift_hi, shift_lo,
        ]
        vec_rows = vec_rows + [jnp.zeros((width,), BF)] * (16 - len(vec_rows))
        scaled = (gain[:, None] * proj).astype(BF)
        first = jnp.concatenate([scaled, jnp.stack(vec_rows)], axis=0)
        rest = jnp.concatenate([output_proj, gate_weight[:, :width], gate_weight[:, width:]], axis=0)
        lead = first.shape[0]

        wh, wht, inv, cotl = prepare(span, base, tok, cot)

        n = width // owners
        if n % 16 == 0:
            along = spread(jnp.concatenate([first, rest], axis=0), "tmc", sizes["tmc"])
            own_first = spread(along[:, :lead], "seq", sizes["seq"]).reshape(chips, lead, width)
            other_first = swap(own_first, "core", 2, 1)
            b, bt, vec = assemble_first(place_s, own_first, other_first)
            own_rest = spread(along[:, lead:], "seq", sizes["seq"]).reshape(chips, -1, width)
            other_rest = swap(own_rest, "core", 2, 1)
        else:
            every = lax.all_gather(first, AXES)
            vec = jnp.concatenate(vector_rows(jnp.sum(every[:, n:].astype(F32), axis=0)), axis=0)
            b = (every[:, :n].reshape(width, width).astype(F32) * vec[2:3]).astype(BF)
            bt = b.T
            every = lax.all_gather(rest, AXES)
            c = every[:, :n].reshape(width, width)
            g = [every[:, k * n : (k + 1) * n].reshape(width, width) for k in (1, 2)]
            g = jnp.concatenate(g, axis=1)
            ct, gt = c.T, g.T

        u, end = drive(wh, b, vec, count)
        rates = vec[1]
        carry = carry_in(end, rates, length, tm_place, sizes, False)
        if n % 16 == 0:
            c, ct, g, gt = assemble_rest(place_s, own_rest, other_rest)
        block_out, st, act, dpre, dm, dst, back_end, sums, bias = middle(
            span, base, u, wh, cotl, tok, carry, vec, c, ct, g, gt
        )
        back = carry_in(back_end, rates, length, tm_place, sizes, True)
        gate_grad, proj_grad = weights(st, act, dpre, dm)
        sums = jnp.sum(sums, axis=0)
        bias = jnp.sum(bias, axis=0)
        small = [by_owner(r, owners) for v in (sums[:width], sums[width:], bias) for r in two_rows(v)]
        small = jnp.concatenate(small, axis=1)
        small = jnp.pad(small, ((0, 0), (0, width - small.shape[1])))[:, None, :]
        pack = jnp.concatenate(
            [
                proj_grad.reshape(owners, -1, width),
                gate_grad[:, :width].reshape(owners, -1, width),
                gate_grad[:, width:].reshape(owners, -1, width),
                jnp.pad(small, ((0, 0), (0, 7), (0, 0))),
            ],
            axis=1,
        )
        early = reduce_to_owner(pack, core, chips)

        adj, m, late = adjoint(dst, u, st, wht, back, carry, vec)
        late = jnp.sum(late.reshape(3, count, width), axis=1)
        col_hi, col_lo = two_rows(late[1])
        small = [
            by_owner(r, owners)
            for v in (late[0, :half], late[0, half:], late[2, :half])
            for r in two_rows(v)
        ]
        small = jnp.concatenate(small, axis=1)
        small = jnp.pad(small, ((0, 0), (0, width - small.shape[1])))[:, None, :]
        cols = jnp.broadcast_to(jnp.stack([col_hi, col_lo])[None], (owners, 2, width))
        pack = jnp.concatenate(
            [m.reshape(owners, -1, width), cols, small, jnp.zeros((owners, 5, width), BF)], axis=1
        )
        final = reduce_to_owner(pack, core, chips)
        tok_grad = inputs_gradient(adj, dm, wh, inv, cot, bt, vec)

        proj_sum = early[:n]
        gate_sum = jnp.concatenate([early[n : 2 * n], early[2 * n : 3 * n]], axis=1)
        row = early[3 * n]
        s1 = row[:n] + row[n : 2 * n]
        s2 = row[2 * n : 3 * n] + row[3 * n : 4 * n]
        bias_sum = row[4 * n : 6 * n] + row[6 * n : 8 * n]
        m_sum = final[:n]
        cols = final[n] + final[n + 1]
        row = final[n + 2]
        q = half // owners
        lam_re_sum = row[:q] + row[q : 2 * q]
        lam_im_sum = row[2 * q : 3 * q] + row[3 * q : 4 * q]
        gamma_grad = row[4 * q : 5 * q] + row[5 * q : 6 * q]
        scale = vec[2]
        in_grad = (gain[:, None] * m_sum + shift[:, None] * cols[None]) * scale[None]
        gain_grad = jnp.sum(m_sum * scale[None] * proj, axis=1) + skip * s1
        shift_grad = jnp.sum((cols * scale)[None] * proj, axis=1) + skip * s2
        skip_grad = gain * s1 + shift * s2
        rate = jnp.exp(decay_log.astype(F32))
        phase = jnp.exp(phase_log.astype(F32))
        modulus = jnp.exp(-rate)
        lam_re = modulus * jnp.cos(phase)
        lam_im = modulus * jnp.sin(phase)
        decay_grad = -rate * (lam_re_sum * lam_re + lam_im_sum * lam_im)
        phase_grad = phase * (lam_im_sum * lam_re - lam_re_sum * lam_im)
        return (
            block_out.reshape(tokens.shape), tok_grad.reshape(tokens.shape), gain_grad, shift_grad,
            in_grad, decay_grad, phase_grad, gamma_grad, proj_sum, skip_grad, gate_sum, bias_sum,
        )

    return body


def solution(mesh):
    seq, tm = mesh.shape["seq"], mesh.shape["tm"]
    fine = Mesh(mesh.devices.reshape(seq, tm // 2, 2), AXES)
    sizes = dict(zip(AXES, (seq, tm // 2, 2)))
    side = P(None, "seq", ("tmc", "core"), None)
    vec = P(AXES)
    mat = P(AXES, None)
    return jax.shard_map(
        make_body(sizes),
        mesh=fine,
        in_specs=(side, P(None, "seq"), side, vec, vec, mat, vec, vec, vec, mat, vec, mat, vec),
        out_specs=(side, side, vec, vec, mat, vec, vec, vec, mat, vec, mat, vec),
        check_vma=False,
    )
```

```python
import math

import jax
import jax.numpy as jnp
from jax import lax
from jax.experimental import pallas as pl
from jax.experimental.pallas import tpu as pltpu
from jax.sharding import Mesh, PartitionSpec as P

F32 = jnp.float32
BF = jnp.bfloat16
AXES = ("seq", "tmc", "core")
GELU_K = math.sqrt(2.0 / math.pi)
VMEM = pl.BlockSpec(memory_space=pltpu.VMEM)
SIDE = 128
AHEAD = 4


def dot(a, b, ca=1, cb=0):
    return lax.dot_general(a, b, (((ca,), (cb,)), ((), ())), preferred_element_type=F32)


def call(body, name, outs, ins, scratch=(), limit=8, far_in=(), far_out=(), copies=0):
    far = pl.BlockSpec(memory_space=pltpu.HBM)
    ins = [
        pltpu.with_memory_space_constraint(a, pltpu.HBM) if k in far_in else a
        for k, a in enumerate(ins)
    ]
    scratch = [pltpu.VMEM(s, t) for s, t in scratch]
    return pl.pallas_call(
        body,
        out_shape=[
            pltpu.HBM(s, t) if k in far_out else jax.ShapeDtypeStruct(s, t)
            for k, (s, t) in enumerate(outs)
        ],
        in_specs=[far if k in far_in else VMEM for k in range(len(ins))],
        out_specs=[far if k in far_out else VMEM for k in range(len(outs))],
        scratch_shapes=scratch + ([pltpu.SemaphoreType.DMA((copies,))] if copies else []),
        compiler_params=pltpu.CompilerParams(vmem_limit_bytes=limit << 20),
        cost_estimate=pl.CostEstimate(flops=0, bytes_accessed=0, transcendentals=0),
        name=name,
    )(*ins)


class Copies:
    def __init__(self, sems):
        self.sems, self.count, self.out = sems, 0, []

    def start(self, src, dest, index):
        copy = pltpu.make_async_copy(src.at[index], dest.at[index], self.sems.at[self.count])
        copy.start()
        self.count += 1
        return copy

    def send(self, src, dest, index):
        self.out.append(self.start(src, dest, index))

    def finish(self):
        for copy in self.out:
            copy.wait()


def time_place():
    return (lax.axis_index("tmc") * 2 + lax.axis_index("core")).astype(jnp.int32)


def device_place():
    seq = lax.axis_index("seq").astype(jnp.int32)
    return seq * (2 * lax.axis_size("tmc")) + time_place()


def split(v):
    high = v.astype(BF)
    return high, (v - high.astype(F32)).astype(BF)


def complex_mul(ar, ai, br, bi):
    return ar * br - ai * bi, ar * bi + ai * br


def complex_step(lr, li, xr, xi, ur, ui):
    return lr * xr - li * xi + ur, lr * xi + li * xr + ui


def lam_rows(vec, count):
    half = vec.shape[1] // 2
    return (
        jnp.broadcast_to(vec[0:1, :half], (count, half)),
        jnp.broadcast_to(vec[0:1, half:], (count, half)),
    )


def swap_order(a, count):
    rows, width = a.shape
    return jnp.swapaxes(a.reshape(rows // count, count, width), 0, 1)


def pack_kernel(*refs):
    far, pack, flag, near, sems = refs[:10], refs[10], refs[11], refs[12:22], refs[22]
    flag[...] = jnp.broadcast_to(lax.axis_index("core").astype(F32), flag.shape)
    copies = [pltpu.make_async_copy(a, b, sems.at[k]) for k, (a, b) in enumerate(zip(far, near))]
    for copy in copies:
        copy.start()
    for copy in copies:
        copy.wait()
    gain, shift, skip, decay, phase, gamma, bias, proj, out_proj, gate = near
    n, width = proj.shape
    half = width // 2
    place = device_place()

    def at(v, size, start):
        length = v.shape[1]
        lane = lax.broadcasted_iota(jnp.int32, (length, size), 1)
        row = lax.broadcasted_iota(jnp.int32, (length, size), 0)
        pick = jnp.where(lane == row + length * place + start, 1.0, 0.0).astype(BF)
        return dot(v[...], pick)

    diag = lax.broadcasted_iota(jnp.int32, (n, n), 0) == lax.broadcasted_iota(jnp.int32, (n, n), 1)
    spread_gain = jnp.where(diag, jnp.broadcast_to(gain[...].astype(F32), (n, n)), 0.0).astype(BF)
    pack[0:n, :] = dot(spread_gain, proj[...]).astype(BF)
    moved = dot(shift[...], proj[...])
    bias_row = at(bias, 2 * width, 0)
    rows = [
        at(gain, width, 0), at(shift, width, 0), at(skip, width, 0),
        at(decay, width, 0) + at(phase, width, half),
        at(gamma, width, 0) + at(gamma, width, half),
        bias_row[:, :width], bias_row[:, width:], moved,
    ]
    pack[n : n + 8, :] = jnp.concatenate(rows, axis=0).astype(BF)
    for k, rest in enumerate((out_proj[...], gate[:, :width], gate[:, width:])):
        pack[(k + 1) * n + 8 : (k + 2) * n + 8, :] = rest


def whiten_kernel(tok, wh_out, inv_far, inv_out, sems):
    copies = Copies(sems)
    count, length, width = tok.shape
    part = 16
    for i in range(0, length, part):
        x = tok[:, i : i + part, :].astype(F32)
        mean = jnp.mean(x, axis=-1, keepdims=True)
        c = x - mean
        inv = lax.rsqrt(jnp.mean(c * c, axis=-1, keepdims=True) + 1e-05)
        rows = slice(i * count, (i + part) * count)
        wh_out[rows, :] = jnp.swapaxes(c * inv, 0, 1).reshape(part * count, width).astype(BF)
        wide = jnp.broadcast_to(inv, (count, part, SIDE))
        inv_out[rows, :] = jnp.swapaxes(wide, 0, 1).reshape(part * count, SIDE)
        if (i + part) % 64 == 0:
            copies.send(inv_out, inv_far, pl.ds((i + part - 64) * count, 64 * count))
    copies.finish()


def live_rows(lengths, start, steps, length, width):
    per, micro = lengths.shape
    used = lengths[...]
    ends = [
        jnp.broadcast_to(used[k : k + 1, m : m + 1], (1, SIDE)) for m in range(micro) for k in range(per)
    ]
    count = len(ends)
    ends = jnp.concatenate(ends, axis=0).reshape(count, 1, SIDE)
    first = time_place() * length + start
    place = first + lax.broadcasted_iota(jnp.int32, (count, steps, SIDE), 1)
    live = jnp.where(place < ends, 1.0, 0.0)
    return jnp.concatenate([live] * (width // SIDE), axis=-1)


def mask_kernel(ends, cot, out):
    count, length, width = cot.shape
    part = 16
    for i in range(0, length, part):
        live = live_rows(ends, i, part, length, width)
        y = jnp.swapaxes(cot[:, i : i + part, :].astype(F32) * live, 0, 1)
        out[i * count : (i + part) * count, :] = y.reshape(part * count, width)


def assemble(dests, own, other, start):
    place = device_place()
    for half, ref in enumerate((own, other)):
        for q in range(own.shape[0]):
            owner = jnp.bitwise_xor(place, 2 * q + half)
            row = pl.multiple_of(owner * 16, 16)
            for k, d in enumerate(dests):
                d[pl.ds(row, 16), :] = ref[q, start + 16 * k : start + 16 * (k + 1), :]


def vector_rows(acc):
    half = acc.shape[1] // 2
    gain, shift, skip = acc[0:1], acc[1:2], acc[2:3]
    rate = jnp.exp(acc[3:4, :half])
    phase = jnp.exp(acc[3:4, half:])
    scale = jnp.exp(acc[4:5])
    modulus = jnp.exp(-rate)
    lam = jnp.concatenate([modulus * jnp.cos(phase), modulus * jnp.sin(phase)], axis=1)
    shifted = acc[7:8] * scale
    bias = 0.5 * acc[5:7]
    return (lam, scale, shifted, skip * gain, skip * shift, bias[0:1], bias[1:2], gain)


def power_rows(lam, length, bits, place):
    half = lam.shape[1] // 2
    re, im = lam[:, :half], lam[:, half:]
    for _ in range(length.bit_length() - 1):
        re, im = complex_mul(re, im, re, im)
    one, zero = jnp.ones_like(re), jnp.zeros_like(re)
    now = {False: (one, zero), True: (one, zero)}
    rows, masks = [], []
    for bit in range(bits):
        taken = lax.rem(lax.shift_right_logical(place, bit), 2) == 1
        rows.append(jnp.concatenate([re, im], axis=1))
        for backward in (False, True):
            later = jnp.logical_not(taken) if backward else taken
            pr, pi = now[backward]
            sign = -1.0 if backward else 1.0
            row = jnp.concatenate([pr, sign * pi], axis=1)
            rows.append(jnp.where(later, row, 0.0))
            nr, ni = complex_mul(pr, pi, re, im)
            now[backward] = (jnp.where(later, nr, pr), jnp.where(later, ni, pi))
        rows.append(jnp.concatenate([re, -im], axis=1))
        masks.append(jnp.where(taken, 1.0, jnp.zeros((1, 2 * half), F32)))
        re, im = complex_mul(re, im, re, im)
    return rows + masks


def drive_body(wh, b, vec, pows, u_out, end_out, bits):
    count, width = end_out.shape
    half = width // 2
    total = wh.shape[0]
    length = total // count
    rows = power_rows(vec[0:1, :], length, bits, time_place())
    for k, r in enumerate(rows):
        pows[k : k + 1, :] = r
    lr, li = lam_rows(vec, count)
    xr = jnp.zeros((count, half), F32)
    xi = xr
    step = 256
    shifted = vec[2:3, :]
    for i in range(0, total, step):
        u_out[i : i + step, :] = dot(wh[i : i + step, :], b[...]) + shifted
        for t in range(i, i + step, count):
            r = slice(t, t + count)
            xr, xi = complex_step(lr, li, xr, xi, u_out[r, :half], u_out[r, half:])
    end_out[:, :half] = xr
    end_out[:, half:] = xi


def drive_gathered_kernel(bits, own, other, wh, b, vec, pows, u_out, end_out):
    acc = jnp.zeros((8, vec.shape[1]), F32)
    for ref in (own, other):
        for q in range(own.shape[0]):
            acc = acc + ref[q, 16:24, :].astype(F32)
    rows = vector_rows(acc)
    for k, r in enumerate(rows):
        vec[k : k + 1, :] = r
    assemble((b,), own, other, 0)
    b[...] = (b[...].astype(F32) * rows[1]).astype(BF)
    drive_body(wh, b, vec, pows, u_out, end_out, bits)


def drive_plain_kernel(bits, b, vec, wh, pows, u_out, end_out):
    drive_body(wh, b, vec, pows, u_out, end_out, bits)


def fold_rows(a, count):
    return jnp.sum(a.reshape(a.shape[0] // count, count, a.shape[1]), axis=0)


def middle_body(
    u, cotl, carry, vec, c, g, wh,
    st, dst, dm_out, y_out, end, sums,
    dm, y, act, dpre, mix, pre, slope, dact, total_grads, sems, put,
):
    count, width = carry.shape
    half = width // 2
    total = u.shape[0]
    rows = 256
    part = 32
    steps = rows // count
    blocks = total // rows
    copies = Copies(sems)
    lr, li = lam_rows(vec, count)
    state = [carry[:, :half], carry[:, half:]]
    zero = jnp.zeros((count, half), F32)
    wide_zero = jnp.zeros((count, width), F32)
    ends_sum = [zero, zero]
    power = [jnp.ones((count, half), F32), zero]
    totals = [wide_zero] * 4
    jump = (lr, -li)
    for _ in range(steps.bit_length() - 1):
        jump = complex_mul(*jump, *jump)

    def block(i):
        return slice(i * rows, (i + 1) * rows)

    def scan(i):
        now = tuple(state)
        for t in range(0, steps, 2):
            r = i * rows + t * count
            mid = r + count
            one = complex_step(lr, li, *now, u[r:mid, :half], u[r:mid, half:])
            last = mid + count
            now = complex_step(lr, li, *one, u[mid:last, :half], u[mid:last, half:])
            st[r:last, :half] = jnp.concatenate([one[0], now[0]], axis=0).astype(BF)
            st[r:last, half:] = jnp.concatenate([one[1], now[1]], axis=0).astype(BF)
        state[:] = now

    def activate(i):
        mix[i % 2] = dot(st[block(i), :], c[...])
        for k in range(0, rows, part):
            r = slice(i * rows + k, i * rows + k + part)
            x = mix[i % 2, k : k + part, :] + (wh[r, :].astype(F32) * vec[3:4, :] + vec[4:5, :])
            sq = x * x
            th = jnp.tanh(x * (GELU_K + (GELU_K * 0.044715) * sq))
            q = 0.5 * th + 0.5
            a = x * q
            act[r, :] = a.astype(BF)
            slope[i % 4, k : k + part, :] = q + a * (1.0 - q) * (
                2.0 * GELU_K + (6.0 * GELU_K * 0.044715) * sq
            )

    def gating(i):
        pre[i % 2] = dot(act[block(i), :], g[...])
        for k in range(0, rows, part):
            r = slice(i * rows + k, i * rows + k + part)
            v = pre[i % 2, k : k + part, :width] + vec[5:6, :]
            h = pre[i % 2, k : k + part, width:] + vec[6:7, :]
            th = jnp.tanh(h)
            vt = v * th
            ct = cotl[r, :]
            dv = ct + ct * th
            dg = dv * (v - vt)
            dpre[r, :width] = dv.astype(BF)
            dpre[r, width:] = dg.astype(BF)
            y[r, :] = (v + vt).astype(BF)
            totals[2] = totals[2] + fold_rows(dv, count)
            totals[3] = totals[3] + fold_rows(dg, count)
        copies.send(y, y_out, pl.ds(i * rows, rows))

    def back(i):
        dact[i % 2] = dot(dpre[block(i), :], g[...], 1, 1)
        for k in range(0, rows, part):
            r = slice(i * rows + k, i * rows + k + part)
            d = dact[i % 2, k : k + part, :] * slope[i % 4, k : k + part, :]
            dm[r, :] = d.astype(BF)
            totals[0] = totals[0] + fold_rows(d * wh[r, :].astype(F32), count)
            totals[1] = totals[1] + fold_rows(d, count)
        copies.send(dm, dm_out, pl.ds(i * rows, rows))

    def ends(i):
        dst[block(i), :] = dot(dm[block(i), :], c[...], 1, 1)
        now = (zero, zero)
        for t in range(steps - 1, -1, -1):
            r = slice(i * rows + t * count, i * rows + (t + 1) * count)
            now = complex_step(lr, -li, *now, dst[r, :half], dst[r, half:])
        ends_sum[:] = complex_step(*power, *now, *ends_sum)
        power[:] = complex_mul(*power, *jump)

    spans = ((0, 2), (2, 4), (4, 6), (6, blocks))
    tiles = [(act, dpre, 0), (act, dpre, width), (st, dm, 0)]
    tasks = []

    def product(first, last, k):
        a, b, start = tiles[k]
        r = slice(first * rows, last * rows)
        value = dot(a[r, :], b[r, start : start + width], 0, 0)
        if first:
            value = value + total_grads[k]
        if last == blocks:
            put(k, value)
        else:
            total_grads[k] = value

    stages = (scan, activate, gating, back, ends)
    for turn in range(blocks + len(stages) - 1):
        for depth in range(len(stages) - 1, -1, -1):
            if 0 <= turn - depth < blocks:
                stages[depth](turn - depth)
            if tasks and depth in (4, 2, 0):
                product(*tasks.pop(0))
        for first, last in spans:
            if turn - 3 == last - 1:
                tasks += [(first, last, k) for k in range(3)]
    for task in tasks:
        product(*task)
    end[:, :half] = ends_sum[0]
    end[:, half:] = ends_sum[1]
    for k, a in enumerate(totals):
        sums[k : k + 1, :] = jnp.sum(a, axis=0, keepdims=True)
    copies.finish()


def owner_of(q, core, crossed=False):
    tmc = lax.axis_size("tmc")
    seq = lax.axis_index("seq").astype(jnp.int32)
    differs = (0, 2 - core, 1 + core, 3)[q // tmc] if crossed else q // tmc
    return (jnp.bitwise_xor(seq, differs) * tmc + q % tmc) * 2 + core


def split_rows(grads, keep, give, index, crossed=False):
    core = lax.axis_index("core").astype(jnp.int32)
    for q in range(keep.shape[0]):
        for ref, side in ((keep, core), (give, 1 - core)):
            row = pl.multiple_of(owner_of(q, side, crossed) * 16, 16)
            ref[q, index : index + 16, :] = grads[pl.ds(row, 16), :]


def middle_gathered_kernel(u, cotl, carry, vec, own, other, wh, *refs):
    outs, scratch = refs[:8], refs[8:]
    *scratch, c, g, grads, sems = scratch
    width = c.shape[0]
    assemble((c, g.at[:, :width], g.at[:, width:]), own, other, 0)
    g[...] = (g[...].astype(F32) * 0.5).astype(BF)

    def put(k, value):
        grads[k] = value.astype(BF)
        split_rows(grads.at[k], outs[6], outs[7], 16 * k, True)

    middle_body(u, cotl, carry, vec, c, g, wh, *outs[:6], *scratch, sems, put)


def middle_plain_kernel(*refs):
    ins, outs, scratch = refs[:7], refs[7:14], refs[14:]
    width = outs[6].shape[0]

    def put(k, value):
        outs[6][:, k * width : (k + 1) * width] = value.astype(BF)

    middle_body(*ins, *outs[:6], *scratch, put)


def output_kernel(ends, y, tok, out, y_in, tok_in, sems):
    count, length, width = tok.shape
    part = 16
    pieces = 4
    step = length // pieces
    copies = Copies(sems)
    waits = [
        (
            copies.start(y, y_in, pl.ds(k * step * count, step * count)),
            copies.start(tok, tok_in, (slice(None), pl.ds(k * step, step))),
        )
        for k in range(pieces)
    ]
    for k in range(pieces):
        for copy in waits[k]:
            copy.wait()
        for i in range(k * step, (k + 1) * step, part):
            live = live_rows(ends, i, part, length, width)
            add = swap_order(y_in[i * count : (i + part) * count, :].astype(F32), count)
            x = tok_in[:, i : i + part, :].astype(F32) + live * add
            tok_in[:, i : i + part, :] = x.astype(BF)
        copies.send(tok_in, out, (slice(None), pl.ds(k * step, step)))
    copies.finish()


def adjoint_body(dst_in, u_in, st_in, wh, back, carry, vec, adj_out, adj, sems):
    count, width = back.shape
    half = width // 2
    total = u_in.shape[0]
    step = 256
    blocks = total // step
    copies = Copies(sems)
    lr, li = lam_rows(vec, count)
    ar, ai = back[:, :half], back[:, half:]
    zero = jnp.zeros((count, half), F32)
    lsr, lsi, gam, csr, csi = zero, zero, zero, zero, zero
    mr, mi = zero, zero
    m = jnp.zeros((width, width), F32)
    for block in range(blocks - 1, -1, -1):
        for t in range(block * step + step - 2 * count, block * step - 1, -2 * count):
            pair = slice(t, t + 2 * count)
            states = st_in[pair, :].astype(F32)
            held = []
            for k in (1, 0):
                r = slice(k * count, (k + 1) * count)
                sr, si = states[r, :half], states[r, half:]
                lsr = lsr + (mr * sr + mi * si)
                lsi = lsi + (mi * sr - mr * si)
                at = slice(t + k * count, t + (k + 1) * count)
                ar, ai = complex_step(lr, -li, ar, ai, dst_in[at, :half], dst_in[at, half:])
                mr, mi = ar, ai
                gam = gam + (ar * u_in[at, :half] + ai * u_in[at, half:])
                csr = csr + ar
                csi = csi + ai
                held.append((ar, ai))
            adj[pair, :half] = jnp.concatenate([held[1][0], held[0][0]], axis=0).astype(BF)
            adj[pair, half:] = jnp.concatenate([held[1][1], held[0][1]], axis=0).astype(BF)
        at = slice(block * step, (block + 1) * step)
        m = m + dot(wh[at, :], adj[at, :], 0, 0)
        copies.send(adj, adj_out, pl.ds(block * step, step))
    cr, ci = carry[:, :half], carry[:, half:]
    lsr = lsr + (ar * cr + ai * ci)
    lsi = lsi + (ai * cr - ar * ci)

    def row(a):
        return jnp.sum(a, axis=0, keepdims=True)

    cols = jnp.concatenate([row(csr), row(csi)], axis=1)
    return copies, m, cols, row(lsr), row(lsi), row(gam)


def by_owner(vectors, owners):
    out = jnp.zeros((owners, SIDE), F32)
    start = 0
    for v in vectors:
        size = v.shape[1]
        n = size // owners
        lane = lax.broadcasted_iota(jnp.int32, (owners, size), 1)
        row = lax.broadcasted_iota(jnp.int32, (owners, size), 0)
        mine = (lane >= row * n) & (lane < row * n + n)
        src = lax.broadcasted_iota(jnp.int32, (size, SIDE), 0)
        dest = lax.broadcasted_iota(jnp.int32, (size, SIDE), 1)
        for part in split(v):
            wide = jnp.where(mine, jnp.broadcast_to(part.astype(F32), (owners, size)), 0.0)
            fold = jnp.where(lax.rem(src, n) + start == dest, 1.0, 0.0)
            out = out + dot(wide.astype(BF), fold.astype(BF))
            start += n
    return out


def adjoint_gathered_kernel(
    dst, u, st, wh, back, carry, vec, sums, adj_out, keep, give,
    adj, grads, small, sems,
):
    width = vec.shape[1]
    owners = 2 * keep.shape[0]
    copies, m, cols, lsr, lsi, gam = adjoint_body(
        dst, u, st, wh, back, carry, vec, adj_out, adj, sems
    )
    bias = jnp.concatenate([sums[2:3, :], sums[3:4, :]], axis=1)
    small[:, :SIDE] = by_owner((lsr, lsi, gam), owners)
    small[:, SIDE:] = by_owner((sums[0:1, :], sums[1:2, :], bias), owners)
    grads[...] = m.astype(BF)
    split_rows(grads, keep, give, 0)
    row_id = lax.broadcasted_iota(jnp.int32, (8, width), 0)
    common = jnp.zeros((8, width), F32)
    for k, piece in enumerate(split(cols)):
        common = jnp.where(row_id == k, piece.astype(F32), common)
    core = lax.axis_index("core").astype(jnp.int32)
    rest = jnp.zeros((1, width - 2 * SIDE), F32)
    for q in range(keep.shape[0]):
        for ref, side in ((keep, core), (give, 1 - core)):
            row = jnp.concatenate([small[pl.ds(owner_of(q, side), 1), :], rest], axis=1)
            ref[q, 16:24, :] = jnp.where(row_id == 2, row, common).astype(BF)
    copies.finish()


def adjoint_plain_kernel(
    dst, u, st, wh, back, carry, vec, adj_out, m_out, rows_out, adj, sems
):
    half = vec.shape[1] // 2
    copies, m, cols, lsr, lsi, gam = adjoint_body(
        dst, u, st, wh, back, carry, vec, adj_out, adj, sems
    )
    m_out[...] = m.astype(BF)
    rows_out[0:1, :] = cols
    rows_out[1:2, :half] = lsr
    rows_out[1:2, half:] = lsi
    rows_out[2:3, :half] = gam
    copies.finish()


def inputs_kernel(adj, dm, cot, inv, wh, b, vec, out, adj_in, dm_in, cot_in, inv_in, buf, sems):
    count, length, width = cot.shape
    rows = 256
    part = 16
    steps = rows // count
    blocks = length * count // rows
    copies = Copies(sems)
    waits = []

    def fetch(i):
        if i < blocks:
            at = pl.ds(i * rows, rows)
            pairs = ((adj, adj_in), (dm, dm_in), (inv, inv_in))
            waits.append([copies.start(src, dest, at) for src, dest in pairs])
            waits[i].append(copies.start(cot, cot_in, (slice(None), pl.ds(i * steps, steps))))

    for i in range(AHEAD):
        fetch(i)
    for i in range(blocks):
        for copy in waits[i]:
            copy.wait()
        fetch(i + AHEAD)
        buf[i % 2] = dot(adj_in[i * rows : (i + 1) * rows, :], b[...], 1, 1)
        for k in range(0, rows, part * count):
            r = slice(i * rows + k, i * rows + k + part * count)
            w = wh[r, :].astype(F32)
            e = buf[i % 2, k : k + part * count, :] + dm_in[r, :].astype(F32) * vec[3:4, :]
            mean = jnp.mean(e, axis=-1, keepdims=True)
            proj = jnp.mean(e * w, axis=-1, keepdims=True)
            wide = jnp.concatenate([inv_in[r, :]] * (width // SIDE), axis=-1)
            d = swap_order((e - mean - w * proj) * wide, count)
            t = slice((i * rows + k) // count, (i * rows + k) // count + part)
            cot_in[:, t, :] = (cot_in[:, t, :].astype(F32) + d).astype(BF)
        copies.send(cot_in, out, (slice(None), pl.ds(i * steps, steps)))
    copies.finish()


def finish_kernel(parts, vec, proj, gain, shift, skip, decay, phase, *refs):
    far, near, sems = refs[:10], refs[10:20], refs[20]
    (
        gate_out, proj_out, in_out, gain_out, shift_out, skip_out, decay_out, phase_out, gamma_out, bias_out,
    ) = near
    n, width = proj.shape
    q = decay.shape[1]
    copies = []

    def ready(*ks):
        for k in ks:
            copies.append(pltpu.make_async_copy(near[k], far[k], sems.at[k]))
            copies[-1].start()

    late = jnp.sum(parts[:, 3 * n :, :].astype(F32), axis=0)
    scale = vec[1:2, :]
    diag = lax.broadcasted_iota(jnp.int32, (n, n), 0) == lax.broadcasted_iota(jnp.int32, (n, n), 1)

    def column(row):
        return jnp.sum(jnp.where(diag, jnp.broadcast_to(row, (n, n)), 0.0), axis=1, keepdims=True)

    def row(col):
        return jnp.sum(jnp.where(diag, jnp.broadcast_to(col, (n, n)), 0.0), axis=0, keepdims=True)

    def take(start, size):
        return small[:, start : start + size] + small[:, start + size : start + 2 * size]

    m = late[:n]
    cols = (late[n : n + 1] + late[n + 1 : n + 2]) * scale
    small = late[n + 2 : n + 3]
    m_scaled = m * scale
    weight = proj[...].astype(F32)
    gains, shifts, skips = (a[...].astype(F32) for a in (gain, shift, skip))
    in_out[...] = column(gains) * m_scaled + column(shifts) * cols
    ready(2)
    s1, s2 = take(SIDE, n), take(SIDE + 2 * n, n)
    gain_out[...] = row(jnp.sum(m_scaled * weight, axis=1, keepdims=True)) + skips * s1
    shift_out[...] = row(jnp.sum(cols * weight, axis=1, keepdims=True)) + skips * s2
    skip_out[...] = gains * s1 + shifts * s2
    bias_out[...] = 0.5 * take(SIDE + 4 * n, 2 * n)
    re, im = take(0, q), take(2 * q, q)
    gamma_out[...] = take(4 * q, q)
    rate = jnp.exp(decay[...].astype(F32))
    turn = jnp.exp(phase[...].astype(F32))
    modulus = jnp.exp(-rate)
    lam_re, lam_im = modulus * jnp.cos(turn), modulus * jnp.sin(turn)
    decay_out[...] = -rate * (re * lam_re + im * lam_im)
    phase_out[...] = turn * (im * lam_re - re * lam_im)
    ready(3, 4, 5, 6, 7, 8, 9)
    early = jnp.sum(parts[:, : 3 * n, :].astype(F32), axis=0)
    gate_out[:, :width] = 0.5 * early[:n]
    gate_out[:, width:] = 0.5 * early[n : 2 * n]
    proj_out[...] = early[2 * n :]
    ready(0, 1)
    for copy in copies:
        copy.wait()


def swap(a, axis, size, bit):
    return lax.ppermute(a, axis, [(k, k ^ bit) for k in range(size)])


def spread(a, axis, size):
    return jnp.stack([a] + [swap(a, axis, size, k) for k in range(1, size)])


def cross_pairs(owners, tmc, turn):
    return [(k, k ^ (2 * tmc << (k % 2 ^ turn))) for k in range(owners)]


def tie(first, *rest):
    return lax.optimization_barrier((first, *rest))


def cmul_rows(row, a):
    half = a.shape[1] // 2
    re, im = complex_mul(row[:half], row[half:], a[:, :half], a[:, half:])
    return jnp.concatenate([re, im], axis=1)


def carry_in(end, pows, bits, sizes, backward, during):
    total, pre = end, jnp.zeros_like(end)
    for bit in range(bits):
        total = during(bit, total)
        if bit == 0:
            got = swap(total, "core", 2, 1)
        else:
            got = swap(total, "tmc", sizes["tmc"], 1 << (bit - 1))
        taken = pows[4 * bits + bit][None]
        later = taken < 0.5 if backward else taken > 0.5
        wide = pows[4 * bit + (3 if backward else 0)]
        pre = pre + cmul_rows(pows[4 * bit + (2 if backward else 1)], got)
        total = jnp.where(later, total, got) + cmul_rows(wide, jnp.where(later, got, total))
    return pre


def add_low(*parts):
    return sum(a.astype(F32) for a in parts).astype(BF)


def make_body(sizes):
    chips = sizes["seq"] * sizes["tmc"]
    owners = chips * 2
    bits = (2 * sizes["tmc"]).bit_length() - 1

    def body(
        tokens, lengths, cotangent, norm_gain, norm_shift, input_proj, decay_log, phase_log,
        gamma_log, output_proj, skip_gain, gate_weight, gate_bias,
    ):
        micro, per, length, width = tokens.shape
        count = micro * per
        total = count * length
        half = width // 2
        n = width // owners
        fast = n % 16 == 0 and sizes["seq"] == 4
        tok = tokens.reshape(count, length, width)
        cot = cotangent.reshape(count, length, width)
        wide_bf, wide_f = ((total, width), BF), ((total, width), F32)

        vectors = (norm_gain, norm_shift, skip_gain, decay_log, phase_log, gamma_log, gate_bias)
        lead = n + 8
        ins = [v.reshape(1, -1) for v in vectors] + [input_proj, output_proj, gate_weight]
        pack, flag = call(
            pack_kernel, "pack", [((4 * n + 8, width), BF), ((1, width), F32)], ins, [(a.shape, BF) for a in ins],
            far_in=range(10) if fast else (), copies=10,
        )

        def whiten(t):
            thin = ((total, SIDE), F32)
            return call(
                whiten_kernel, "whiten", [wide_bf, thin], (t,), [thin], far_out=(1,), copies=length // 64
            )

        def mask(ct):
            return call(mask_kernel, "mask", [wide_f], (lengths.T, ct))[0]

        powers = ((-(-5 * bits // 8) * 8, width), F32)
        if fast:
            along = spread(pack, "tmc", sizes["tmc"])
            wh, inv = whiten(tok)
            along, wh = tie(along, wh)
            own_first = spread(along[:, :lead], "seq", sizes["seq"]).reshape(chips, lead, width)
            rest = along[:, lead:]
            rest = [rest] + [swap(rest, "seq", sizes["seq"], k) for k in (1, 2)]
            own_first, *rest = tie(own_first, *rest)
            other_first = swap(own_first, "core", 2, 1)
            forward = jnp.where(flag > 0.5, rest[2], rest[1])
            rest.append(lax.ppermute(forward, AXES, cross_pairs(owners, sizes["tmc"], 1)))
            b, vec, pows, u, end = call(
                lambda *r: drive_gathered_kernel(bits, *r), "drive",
                [((width, width), BF), ((8, width), F32), powers, wide_f, ((count, width), F32)],
                (own_first, other_first, wh),
            )
        else:
            wh, inv = whiten(tok)
            cotl = mask(cot)
            every = lax.all_gather(pack, AXES)
            vec = jnp.sum(every[:, n:lead].astype(F32), axis=0)
            vec = jnp.concatenate(vector_rows(vec), axis=0)
            mats = [every[:, :n]] + [every[:, lead + k * n : lead + (k + 1) * n] for k in range(3)]
            mats = [a.reshape(width, width) for a in mats]
            b = (mats[0].astype(F32) * vec[1:2]).astype(BF)
            c = mats[1]
            g = (jnp.concatenate(mats[2:], axis=1).astype(F32) * 0.5).astype(BF)
            pows, u, end = call(
                lambda *r: drive_plain_kernel(bits, *r), "drive",
                [powers, wide_f, ((count, width), F32)], (b, vec, wh),
            )

        held = {}

        def early_rest(bit, a):
            if fast and bit == 1:
                a, rest[3], late_cot = tie(a, rest[3], cot)
                held["cotl"] = mask(late_cot)
            if fast and bit == 2:
                a, held["cotl"] = tie(a, held["cotl"])
                parts = tie(a, *rest)[1:]
                held["own"] = jnp.stack(parts).reshape(chips, -1, width)
                held["other"] = swap(held["own"], "core", 2, 1)
            return a

        carry = carry_in(end, pows, bits, sizes, False, early_rest)
        if fast:
            cotl = held["cotl"]
        rows = 256
        blocks = total // rows
        side = ((count, length, width), BF)
        outs = [wide_bf, wide_f, wide_bf, wide_bf, ((count, width), F32), ((4, width), F32)]
        scratch = [wide_bf] * 3 + [
            ((total, 2 * width), BF), ((2, rows, width), F32), ((2, rows, 2 * width), F32),
            ((4, rows, width), F32), ((2, rows, width), F32), ((3, width, width), F32),
        ]
        if fast:
            ins = (u, cotl, carry, vec, held["own"], held["other"], wh)
            st, dst, dm, y, back_end, sums, keep, give = call(
                middle_gathered_kernel, "middle", outs + [((chips, 48, width), BF)] * 2, ins,
                scratch + [((width, width), BF), ((width, 2 * width), BF), ((3, width, width), BF)], limit=32, far_out=(2, 3), copies=2 * blocks,
            )
        else:
            st, dst, dm, y, back_end, sums, out_grads = call(
                middle_plain_kernel, "middle", outs + [((width, 3 * width), BF)],
                (u, cotl, carry, vec, c, g, wh), scratch,
                limit=32, far_out=(2, 3), copies=2 * blocks,
            )


        def seq_parts(both):
            both = both.reshape(sizes["seq"], sizes["tmc"], -1, width)
            return [both[0]] + [swap(both[k], "seq", sizes["seq"], k) for k in range(1, sizes["seq"])]

        def early_sums(bit, a):
            if fast and bit == 2:
                got = swap(give, "core", 2, 1)
                low, high = slice(0, chips // 2), slice(chips // 2, chips)
                high = add_low(keep[high], got[high])
                low = add_low(keep[low], got[low])
                a, high, low = tie(a, high, low)
                got = lax.ppermute(high, AXES, cross_pairs(owners, sizes["tmc"], 0))
                held["early"] = (low, got)
            return a

        back = carry_in(back_end, pows, bits, sizes, True, early_sums)

        ins = (dst, u, st, wh, back, carry, vec)
        if fast:
            adj, late_keep, late_give = call(
                adjoint_gathered_kernel, "adjoint",
                [wide_bf] + [((chips, 24, width), BF)] * 2, (*ins, sums),
                [wide_bf] + [((width, width), BF), ((owners, 2 * SIDE), F32)],
                limit=10, far_out=(0,), copies=blocks,
            )
            quarter = chips // 4
            low, high = (
                add_low(*(a[k : k + quarter] for a in held["early"])) for k in (0, quarter)
            )
            low, high, late_keep, late_give = tie(low, high, late_keep, late_give)
            early = add_low(low, lax.ppermute(high, AXES, cross_pairs(owners, sizes["tmc"], 1)))
            late = add_low(late_keep, swap(late_give, "core", 2, 1))
            late, y = tie(late, y)
            both = jnp.concatenate([early, add_low(*seq_parts(late))], axis=1)
            block_out = call(
                output_kernel, "output", [side], (lengths.T, y, tok), [wide_bf, side],
                limit=8, far_in=(1, 2), far_out=(0,), copies=12,
            )[0]
            both, adj, block_out = tie(both, adj, block_out)
            both = lax.all_to_all(both, "tmc", 0, 0)
        else:
            adj, m, late_rows = call(
                adjoint_plain_kernel, "adjoint",
                [wide_bf, ((width, width), BF), ((8, width), F32)], ins, [wide_bf],
                limit=10, far_out=(0,), copies=blocks,
            )
            block_out = call(
                output_kernel, "output", [side], (lengths.T, y, tok), [wide_bf, side],
                limit=8, far_in=(1, 2), far_out=(0,), copies=12,
            )[0]
        (tok_grad,) = call(
            inputs_kernel, "inputs", [side], (adj, dm, cot, inv, wh, b, vec),
            [wide_bf, wide_bf, side, ((total, SIDE), F32), ((2, rows, width), F32)],
            limit=14, far_in=range(4), far_out=(0,), copies=5 * blocks,
        )

        q = half // owners
        if fast:
            shapes = [(n, 2 * width), (n, width), (n, width)] + [(1, n)] * 3 + [(1, q)] * 3 + [(1, 2 * n)]
            shapes = [(a, F32) for a in shapes]
            rows = [v.reshape(1, -1) for v in (norm_gain, norm_shift, skip_gain, decay_log, phase_log)]
            grads = call(
                finish_kernel, "finish", shapes, (both, vec, input_proj, *rows), shapes,
                far_out=range(10), copies=10,
            )
            gate_sum, proj_sum, in_grad = grads[:3]
            gain_grad, shift_grad, skip_grad, decay_grad, phase_grad, gamma_grad, bias_sum = (
                a.reshape(-1) for a in grads[3:]
            )
        else:
            def scatter(a):
                return lax.psum_scatter(a.astype(F32), AXES, scatter_dimension=0, tiled=True)

            gate_sum = scatter(out_grads[:, : 2 * width]) * 0.5
            proj_sum = scatter(out_grads[:, 2 * width :])
            m_sum = scatter(m)
            cols = lax.psum(late_rows[0], AXES)
            lam_re_sum = scatter(late_rows[1, :half])
            lam_im_sum = scatter(late_rows[1, half:])
            gamma_grad = scatter(late_rows[2, :half])
            s1, s2 = scatter(sums[0]), scatter(sums[1])
            bias_sum = scatter(sums[2:].reshape(2 * width)) * 0.5
            gain = norm_gain.astype(F32)
            shift = norm_shift.astype(F32)
            skip = skip_gain.astype(F32)
            proj = input_proj.astype(F32)
            scale = vec[1]
            in_grad = (gain[:, None] * m_sum + shift[:, None] * cols[None]) * scale[None]
            gain_grad = jnp.sum(m_sum * scale[None] * proj, axis=1) + skip * s1
            shift_grad = jnp.sum((cols * scale)[None] * proj, axis=1) + skip * s2
            skip_grad = gain * s1 + shift * s2
            rate = jnp.exp(decay_log.astype(F32))
            phase = jnp.exp(phase_log.astype(F32))
            modulus = jnp.exp(-rate)
            lam_re = modulus * jnp.cos(phase)
            lam_im = modulus * jnp.sin(phase)
            decay_grad = -rate * (lam_re_sum * lam_re + lam_im_sum * lam_im)
            phase_grad = phase * (lam_im_sum * lam_re - lam_re_sum * lam_im)
        return (
            block_out.reshape(tokens.shape), tok_grad.reshape(tokens.shape), gain_grad, shift_grad,
            in_grad, decay_grad, phase_grad, gamma_grad, proj_sum, skip_grad, gate_sum, bias_sum,
        )

    return body


def solution(mesh):
    seq, tm = mesh.shape["seq"], mesh.shape["tm"]
    fine = Mesh(mesh.devices.reshape(seq, tm // 2, 2), AXES)
    sizes = dict(zip(AXES, (seq, tm // 2, 2)))
    side = P(None, "seq", ("tmc", "core"), None)
    vec = P(AXES)
    mat = P(AXES, None)
    return jax.shard_map(
        make_body(sizes),
        mesh=fine,
        in_specs=(side, P(None, "seq"), side, vec, vec, mat, vec, vec, vec, mat, vec, mat, vec),
        out_specs=(side, side, vec, vec, mat, vec, vec, vec, mat, vec, mat, vec),
        check_vma=False,
    )
```

```python
import math

import jax
import jax.numpy as jnp
from jax import lax
from jax.experimental import pallas as pl
from jax.experimental.pallas import tpu as pltpu
from jax.sharding import Mesh, PartitionSpec as P

F32 = jnp.float32
BF = jnp.bfloat16
AXES = ("seq", "tmc", "core")
GELU_K = math.sqrt(2.0 / math.pi)
VMEM = pl.BlockSpec(memory_space=pltpu.VMEM)
SIDE = 128
AHEAD = 4


def dot(a, b, ca=1, cb=0):
    return lax.dot_general(a, b, (((ca,), (cb,)), ((), ())), preferred_element_type=F32)


def call(body, name, outs, ins, scratch=(), limit=8, far_in=(), far_out=(), copies=0):
    far = pl.BlockSpec(memory_space=pltpu.HBM)
    ins = [
        pltpu.with_memory_space_constraint(a, pltpu.HBM) if k in far_in else a
        for k, a in enumerate(ins)
    ]
    scratch = [pltpu.VMEM(s, t) for s, t in scratch]
    return pl.pallas_call(
        body,
        out_shape=[
            pltpu.HBM(s, t) if k in far_out else jax.ShapeDtypeStruct(s, t)
            for k, (s, t) in enumerate(outs)
        ],
        in_specs=[far if k in far_in else VMEM for k in range(len(ins))],
        out_specs=[far if k in far_out else VMEM for k in range(len(outs))],
        scratch_shapes=scratch + ([pltpu.SemaphoreType.DMA((copies,))] if copies else []),
        compiler_params=pltpu.CompilerParams(vmem_limit_bytes=limit << 20),
        cost_estimate=pl.CostEstimate(flops=0, bytes_accessed=0, transcendentals=0),
        name=name,
    )(*ins)


class Copies:
    def __init__(self, sems):
        self.sems, self.count, self.out = sems, 0, []

    def start(self, src, dest, index):
        copy = pltpu.make_async_copy(src.at[index], dest.at[index], self.sems.at[self.count])
        copy.start()
        self.count += 1
        return copy

    def send(self, src, dest, index):
        self.out.append(self.start(src, dest, index))

    def finish(self):
        for copy in self.out:
            copy.wait()


def time_place():
    return (lax.axis_index("tmc") * 2 + lax.axis_index("core")).astype(jnp.int32)


def device_place():
    seq = lax.axis_index("seq").astype(jnp.int32)
    return seq * (2 * lax.axis_size("tmc")) + time_place()


def split(v):
    high = v.astype(BF)
    return high, (v - high.astype(F32)).astype(BF)


def complex_mul(ar, ai, br, bi):
    return ar * br - ai * bi, ar * bi + ai * br


def complex_step(lr, li, xr, xi, ur, ui):
    return lr * xr - li * xi + ur, lr * xi + li * xr + ui


def lam_rows(vec, count):
    half = vec.shape[1] // 2
    return (
        jnp.broadcast_to(vec[0:1, :half], (count, half)),
        jnp.broadcast_to(vec[0:1, half:], (count, half)),
    )


def swap_order(a, count):
    rows, width = a.shape
    return jnp.swapaxes(a.reshape(rows // count, count, width), 0, 1)


def pack_kernel(*refs):
    far, pack, flag, near, sems = refs[:10], refs[10], refs[11], refs[12:22], refs[22]
    flag[...] = jnp.broadcast_to(lax.axis_index("core").astype(F32), flag.shape)
    copies = [pltpu.make_async_copy(a, b, sems.at[k]) for k, (a, b) in enumerate(zip(far, near))]
    for copy in copies:
        copy.start()
    for copy in copies:
        copy.wait()
    gain, shift, skip, decay, phase, gamma, bias, proj, out_proj, gate = near
    n, width = proj.shape
    half = width // 2
    place = device_place()

    def at(v, size, start):
        length = v.shape[1]
        lane = lax.broadcasted_iota(jnp.int32, (length, size), 1)
        row = lax.broadcasted_iota(jnp.int32, (length, size), 0)
        pick = jnp.where(lane == row + length * place + start, 1.0, 0.0).astype(BF)
        return dot(v[...], pick)

    diag = lax.broadcasted_iota(jnp.int32, (n, n), 0) == lax.broadcasted_iota(jnp.int32, (n, n), 1)
    spread_gain = jnp.where(diag, jnp.broadcast_to(gain[...].astype(F32), (n, n)), 0.0).astype(BF)
    pack[0:n, :] = dot(spread_gain, proj[...]).astype(BF)
    moved = dot(shift[...], proj[...])
    bias_row = at(bias, 2 * width, 0)
    rows = [
        at(gain, width, 0), at(shift, width, 0), at(skip, width, 0),
        at(decay, width, 0) + at(phase, width, half),
        at(gamma, width, 0) + at(gamma, width, half),
        bias_row[:, :width], bias_row[:, width:], moved,
    ]
    pack[n : n + 8, :] = jnp.concatenate(rows, axis=0).astype(BF)
    for k, rest in enumerate((out_proj[...], gate[:, :width], gate[:, width:])):
        pack[(k + 1) * n + 8 : (k + 2) * n + 8, :] = rest


def whiten_kernel(tok, wh_out, inv_far, inv_out, sems):
    copies = Copies(sems)
    count, length, width = tok.shape
    part = 16
    for i in range(0, length, part):
        x = tok[:, i : i + part, :].astype(F32)
        mean = jnp.mean(x, axis=-1, keepdims=True)
        c = x - mean
        inv = lax.rsqrt(jnp.mean(c * c, axis=-1, keepdims=True) + 1e-05)
        rows = slice(i * count, (i + part) * count)
        wh_out[rows, :] = jnp.swapaxes(c * inv, 0, 1).reshape(part * count, width).astype(BF)
        wide = jnp.broadcast_to(inv, (count, part, SIDE))
        inv_out[rows, :] = jnp.swapaxes(wide, 0, 1).reshape(part * count, SIDE)
        if (i + part) % 64 == 0:
            copies.send(inv_out, inv_far, pl.ds((i + part - 64) * count, 64 * count))
    copies.finish()


def live_rows(lengths, start, steps, length, width):
    per, micro = lengths.shape
    used = lengths[...]
    ends = [
        jnp.broadcast_to(used[k : k + 1, m : m + 1], (1, SIDE)) for m in range(micro) for k in range(per)
    ]
    count = len(ends)
    ends = jnp.concatenate(ends, axis=0).reshape(count, 1, SIDE)
    first = time_place() * length + start
    place = first + lax.broadcasted_iota(jnp.int32, (count, steps, SIDE), 1)
    live = jnp.where(place < ends, 1.0, 0.0)
    return jnp.concatenate([live] * (width // SIDE), axis=-1)


def mask_kernel(ends, cot, out):
    count, length, width = cot.shape
    part = 16
    for i in range(0, length, part):
        live = live_rows(ends, i, part, length, width)
        y = jnp.swapaxes(cot[:, i : i + part, :].astype(F32) * live, 0, 1)
        out[i * count : (i + part) * count, :] = y.reshape(part * count, width)


def assemble(dests, own, other, start):
    place = device_place()
    for half, ref in enumerate((own, other)):
        for q in range(own.shape[0]):
            owner = jnp.bitwise_xor(place, 2 * q + half)
            row = pl.multiple_of(owner * 16, 16)
            for k, d in enumerate(dests):
                d[pl.ds(row, 16), :] = ref[q, start + 16 * k : start + 16 * (k + 1), :]


def vector_rows(acc):
    half = acc.shape[1] // 2
    gain, shift, skip = acc[0:1], acc[1:2], acc[2:3]
    rate = jnp.exp(acc[3:4, :half])
    phase = jnp.exp(acc[3:4, half:])
    scale = jnp.exp(acc[4:5])
    modulus = jnp.exp(-rate)
    lam = jnp.concatenate([modulus * jnp.cos(phase), modulus * jnp.sin(phase)], axis=1)
    shifted = acc[7:8] * scale
    bias = 0.5 * acc[5:7]
    return (lam, scale, shifted, skip * gain, skip * shift, bias[0:1], bias[1:2], gain)


def power_rows(lam, length, bits, place):
    half = lam.shape[1] // 2
    re, im = lam[:, :half], lam[:, half:]
    for _ in range(length.bit_length() - 1):
        re, im = complex_mul(re, im, re, im)
    one, zero = jnp.ones_like(re), jnp.zeros_like(re)
    now = {False: (one, zero), True: (one, zero)}
    rows, masks = [], []
    for bit in range(bits):
        taken = lax.rem(lax.shift_right_logical(place, bit), 2) == 1
        rows.append(jnp.concatenate([re, im], axis=1))
        for backward in (False, True):
            later = jnp.logical_not(taken) if backward else taken
            pr, pi = now[backward]
            sign = -1.0 if backward else 1.0
            row = jnp.concatenate([pr, sign * pi], axis=1)
            rows.append(jnp.where(later, row, 0.0))
            nr, ni = complex_mul(pr, pi, re, im)
            now[backward] = (jnp.where(later, nr, pr), jnp.where(later, ni, pi))
        rows.append(jnp.concatenate([re, -im], axis=1))
        masks.append(jnp.where(taken, 1.0, jnp.zeros((1, 2 * half), F32)))
        re, im = complex_mul(re, im, re, im)
    return rows + masks


def drive_body(wh, b, vec, pows, u_out, end_out, bits):
    count, width = end_out.shape
    half = width // 2
    total = wh.shape[0]
    length = total // count
    rows = power_rows(vec[0:1, :], length, bits, time_place())
    for k, r in enumerate(rows):
        pows[k : k + 1, :] = r
    lr, li = lam_rows(vec, count)
    xr = jnp.zeros((count, half), F32)
    xi = xr
    step = 256
    shifted = vec[2:3, :]
    for i in range(0, total, step):
        u_out[i : i + step, :] = dot(wh[i : i + step, :], b[...]) + shifted
        for t in range(i, i + step, count):
            r = slice(t, t + count)
            xr, xi = complex_step(lr, li, xr, xi, u_out[r, :half], u_out[r, half:])
    end_out[:, :half] = xr
    end_out[:, half:] = xi


def drive_gathered_kernel(bits, own, other, wh, b, vec, pows, u_out, end_out):
    acc = jnp.zeros((8, vec.shape[1]), F32)
    for ref in (own, other):
        for q in range(own.shape[0]):
            acc = acc + ref[q, 16:24, :].astype(F32)
    rows = vector_rows(acc)
    for k, r in enumerate(rows):
        vec[k : k + 1, :] = r
    assemble((b,), own, other, 0)
    b[...] = (b[...].astype(F32) * rows[1]).astype(BF)
    drive_body(wh, b, vec, pows, u_out, end_out, bits)


def drive_plain_kernel(bits, b, vec, wh, pows, u_out, end_out):
    drive_body(wh, b, vec, pows, u_out, end_out, bits)


def fold_rows(a, count):
    return jnp.sum(a.reshape(a.shape[0] // count, count, a.shape[1]), axis=0)


def middle_body(
    u, cotl, carry, vec, c, g, wh,
    st, dst, act, dpre, dm, y, end, sums,
    mix, pre, slope, dact,
):
    count, width = carry.shape
    half = width // 2
    total = u.shape[0]
    rows = 256
    part = 32
    steps = rows // count
    blocks = total // rows
    lr, li = lam_rows(vec, count)
    state = [carry[:, :half], carry[:, half:]]
    zero = jnp.zeros((count, half), F32)
    wide_zero = jnp.zeros((count, width), F32)
    ends_sum = [zero, zero]
    power = [jnp.ones((count, half), F32), zero]
    totals = [wide_zero] * 4
    jump = (lr, -li)
    for _ in range(steps.bit_length() - 1):
        jump = complex_mul(*jump, *jump)

    def block(i):
        return slice(i * rows, (i + 1) * rows)

    def scan(i):
        now = tuple(state)
        for t in range(0, steps, 2):
            r = i * rows + t * count
            mid = r + count
            one = complex_step(lr, li, *now, u[r:mid, :half], u[r:mid, half:])
            last = mid + count
            now = complex_step(lr, li, *one, u[mid:last, :half], u[mid:last, half:])
            st[r:last, :half] = jnp.concatenate([one[0], now[0]], axis=0).astype(BF)
            st[r:last, half:] = jnp.concatenate([one[1], now[1]], axis=0).astype(BF)
        state[:] = now

    def activate(i):
        mix[i % 2] = dot(st[block(i), :], c[...])
        for k in range(0, rows, part):
            r = slice(i * rows + k, i * rows + k + part)
            x = mix[i % 2, k : k + part, :] + (wh[r, :].astype(F32) * vec[3:4, :] + vec[4:5, :])
            sq = x * x
            th = jnp.tanh(x * (GELU_K + (GELU_K * 0.044715) * sq))
            q = 0.5 * th + 0.5
            a = x * q
            act[r, :] = a.astype(BF)
            slope[i % 4, k : k + part, :] = q + a * (1.0 - q) * (
                2.0 * GELU_K + (6.0 * GELU_K * 0.044715) * sq
            )

    def gating(i):
        pre[i % 2] = dot(act[block(i), :], g[...])
        for k in range(0, rows, part):
            r = slice(i * rows + k, i * rows + k + part)
            v = pre[i % 2, k : k + part, :width] + vec[5:6, :]
            h = pre[i % 2, k : k + part, width:] + vec[6:7, :]
            th = jnp.tanh(h)
            vt = v * th
            ct = cotl[r, :]
            dv = ct + ct * th
            dg = dv * (v - vt)
            dpre[r, :width] = dv.astype(BF)
            dpre[r, width:] = dg.astype(BF)
            y[r, :] = (v + vt).astype(BF)
            totals[2] = totals[2] + fold_rows(dv, count)
            totals[3] = totals[3] + fold_rows(dg, count)

    def back(i):
        dact[i % 2] = dot(dpre[block(i), :], g[...], 1, 1)
        for k in range(0, rows, part):
            r = slice(i * rows + k, i * rows + k + part)
            d = dact[i % 2, k : k + part, :] * slope[i % 4, k : k + part, :]
            dm[r, :] = d.astype(BF)
            totals[0] = totals[0] + fold_rows(d * wh[r, :].astype(F32), count)
            totals[1] = totals[1] + fold_rows(d, count)

    def ends(i):
        dst[block(i), :] = dot(dm[block(i), :], c[...], 1, 1)
        now = (zero, zero)
        for t in range(steps - 1, -1, -1):
            r = slice(i * rows + t * count, i * rows + (t + 1) * count)
            now = complex_step(lr, -li, *now, dst[r, :half], dst[r, half:])
        ends_sum[:] = complex_step(*power, *now, *ends_sum)
        power[:] = complex_mul(*power, *jump)

    stages = (scan, activate, gating, back, ends)
    for turn in range(blocks + len(stages) - 1):
        for depth in range(len(stages) - 1, -1, -1):
            if 0 <= turn - depth < blocks:
                stages[depth](turn - depth)
    end[:, :half] = ends_sum[0]
    end[:, half:] = ends_sum[1]
    for k, a in enumerate(totals):
        sums[k : k + 1, :] = jnp.sum(a, axis=0, keepdims=True)


def owner_of(q, core, crossed=False):
    tmc = lax.axis_size("tmc")
    seq = lax.axis_index("seq").astype(jnp.int32)
    differs = (0, 2 - core, 1 + core, 3)[q // tmc] if crossed else q // tmc
    along = jnp.bitwise_xor(lax.axis_index("tmc").astype(jnp.int32), q % tmc)
    return (jnp.bitwise_xor(seq, differs) * tmc + along) * 2 + core


def split_rows(grads, keep, give, index, crossed=False):
    core = lax.axis_index("core").astype(jnp.int32)
    for q in range(keep.shape[0]):
        for ref, side in ((keep, core), (give, 1 - core)):
            row = pl.multiple_of(owner_of(q, side, crossed) * 16, 16)
            ref[q, index : index + 16, :] = grads[pl.ds(row, 16), :]


def middle_gathered_kernel(u, cotl, carry, vec, own, other, wh, *refs):
    *refs, c, g = refs
    width = c.shape[0]
    assemble((c, g.at[:, :width], g.at[:, width:]), own, other, 0)
    g[...] = (g[...].astype(F32) * 0.5).astype(BF)
    middle_body(u, cotl, carry, vec, c, g, wh, *refs)


def weight_products(act, dpre, st, dm):
    width = st.shape[1]
    for k, (a, b, start) in enumerate(((act, dpre, 0), (act, dpre, width), (st, dm, 0))):
        yield k, dot(a[...], b[:, start : start + width], 0, 0).astype(BF)


def weights_gathered_kernel(act, dpre, st, dm, keep, give, grads):
    for k, value in weight_products(act, dpre, st, dm):
        grads[k] = value
        split_rows(grads.at[k], keep, give, 16 * k, True)


def weights_plain_kernel(act, dpre, st, dm, out):
    width = st.shape[1]
    for k, value in weight_products(act, dpre, st, dm):
        out[:, k * width : (k + 1) * width] = value


def output_kernel(lengths, y, tok, out, buf, sems):
    count, length, width = tok.shape
    part = 16
    pieces = 4
    step = length // pieces
    copies = Copies(sems)
    for k in range(pieces):
        for i in range(k * step, (k + 1) * step, part):
            live = live_rows(lengths, i, part, length, width)
            add = swap_order(y[i * count : (i + part) * count, :].astype(F32), count)
            buf[:, i : i + part, :] = (tok[:, i : i + part, :].astype(F32) + live * add).astype(BF)
        copies.send(buf, out, (slice(None), pl.ds(k * step, step)))
    copies.finish()


def adjoint_body(dst_in, u_in, st_in, wh, back, carry, vec, adj):
    count, width = back.shape
    half = width // 2
    total = u_in.shape[0]
    step = 256
    blocks = total // step
    lr, li = lam_rows(vec, count)
    ar, ai = back[:, :half], back[:, half:]
    zero = jnp.zeros((count, half), F32)
    lsr, lsi, gam, csr, csi = zero, zero, zero, zero, zero
    mr, mi = zero, zero
    m = jnp.zeros((width, width), F32)
    for block in range(blocks - 1, -1, -1):
        for t in range(block * step + step - 2 * count, block * step - 1, -2 * count):
            pair = slice(t, t + 2 * count)
            states = st_in[pair, :].astype(F32)
            held = []
            for k in (1, 0):
                r = slice(k * count, (k + 1) * count)
                sr, si = states[r, :half], states[r, half:]
                lsr = lsr + (mr * sr + mi * si)
                lsi = lsi + (mi * sr - mr * si)
                at = slice(t + k * count, t + (k + 1) * count)
                ar, ai = complex_step(lr, -li, ar, ai, dst_in[at, :half], dst_in[at, half:])
                mr, mi = ar, ai
                gam = gam + (ar * u_in[at, :half] + ai * u_in[at, half:])
                csr = csr + ar
                csi = csi + ai
                held.append((ar, ai))
            adj[pair, :half] = jnp.concatenate([held[1][0], held[0][0]], axis=0).astype(BF)
            adj[pair, half:] = jnp.concatenate([held[1][1], held[0][1]], axis=0).astype(BF)
        at = slice(block * step, (block + 1) * step)
        m = m + dot(wh[at, :], adj[at, :], 0, 0)
    cr, ci = carry[:, :half], carry[:, half:]
    lsr = lsr + (ar * cr + ai * ci)
    lsi = lsi + (ai * cr - ar * ci)

    def row(a):
        return jnp.sum(a, axis=0, keepdims=True)

    cols = jnp.concatenate([row(csr), row(csi)], axis=1)
    return m, cols, row(lsr), row(lsi), row(gam)


def by_owner(vectors, owners):
    out = jnp.zeros((owners, SIDE), F32)
    start = 0
    for v in vectors:
        size = v.shape[1]
        n = size // owners
        lane = lax.broadcasted_iota(jnp.int32, (owners, size), 1)
        row = lax.broadcasted_iota(jnp.int32, (owners, size), 0)
        mine = (lane >= row * n) & (lane < row * n + n)
        src = lax.broadcasted_iota(jnp.int32, (size, SIDE), 0)
        dest = lax.broadcasted_iota(jnp.int32, (size, SIDE), 1)
        for part in split(v):
            wide = jnp.where(mine, jnp.broadcast_to(part.astype(F32), (owners, size)), 0.0)
            fold = jnp.where(lax.rem(src, n) + start == dest, 1.0, 0.0)
            out = out + dot(wide.astype(BF), fold.astype(BF))
            start += n
    return out


def adjoint_gathered_kernel(
    dst, u, st, wh, back, carry, vec, sums, adj, keep, give, grads, small,
):
    width = vec.shape[1]
    owners = 2 * keep.shape[0]
    m, cols, lsr, lsi, gam = adjoint_body(
        dst, u, st, wh, back, carry, vec, adj
    )
    bias = jnp.concatenate([sums[2:3, :], sums[3:4, :]], axis=1)
    small[:, :SIDE] = by_owner((lsr, lsi, gam), owners)
    small[:, SIDE:] = by_owner((sums[0:1, :], sums[1:2, :], bias), owners)
    grads[...] = m.astype(BF)
    split_rows(grads, keep, give, 0)
    row_id = lax.broadcasted_iota(jnp.int32, (8, width), 0)
    common = jnp.zeros((8, width), F32)
    for k, piece in enumerate(split(cols)):
        common = jnp.where(row_id == k, piece.astype(F32), common)
    core = lax.axis_index("core").astype(jnp.int32)
    rest = jnp.zeros((1, width - 2 * SIDE), F32)
    for q in range(keep.shape[0]):
        for ref, side in ((keep, core), (give, 1 - core)):
            row = jnp.concatenate([small[pl.ds(owner_of(q, side), 1), :], rest], axis=1)
            ref[q, 16:24, :] = jnp.where(row_id == 2, row, common).astype(BF)


def adjoint_plain_kernel(
    dst, u, st, wh, back, carry, vec, adj, m_out, rows_out
):
    half = vec.shape[1] // 2
    m, cols, lsr, lsi, gam = adjoint_body(
        dst, u, st, wh, back, carry, vec, adj
    )
    m_out[...] = m.astype(BF)
    rows_out[0:1, :] = cols
    rows_out[1:2, :half] = lsr
    rows_out[1:2, half:] = lsi
    rows_out[2:3, :half] = gam


def inputs_kernel(adj, dm, cot, inv, wh, b, vec, out, res, buf, sems):
    count, length, width = cot.shape
    rows = 256
    part = 16
    steps = rows // count
    copies = Copies(sems)
    for i in range(length * count // rows):
        buf[i % 2] = dot(adj[i * rows : (i + 1) * rows, :], b[...], 1, 1)
        for k in range(0, rows, part * count):
            r = slice(i * rows + k, i * rows + k + part * count)
            w = wh[r, :].astype(F32)
            e = buf[i % 2, k : k + part * count, :] + dm[r, :].astype(F32) * vec[3:4, :]
            mean = jnp.mean(e, axis=-1, keepdims=True)
            proj = jnp.mean(e * w, axis=-1, keepdims=True)
            wide = jnp.concatenate([inv[r, :]] * (width // SIDE), axis=-1)
            d = swap_order((e - mean - w * proj) * wide, count)
            t = slice((i * rows + k) // count, (i * rows + k) // count + part)
            res[:, t, :] = (cot[:, t, :].astype(F32) + d).astype(BF)
        copies.send(res, out, (slice(None), pl.ds(i * steps, steps)))
    copies.finish()


def finish_kernel(vec, proj, gain, shift, skip, decay, phase, *refs):
    *parts, sems = refs
    parts, far, near = parts[:-20], parts[-20:-10], parts[-10:]
    (
        gate_out, proj_out, in_out, gain_out, shift_out, skip_out, decay_out, phase_out, gamma_out, bias_out,
    ) = near
    n, width = proj.shape
    q = decay.shape[1]
    copies = []

    def ready(*ks):
        for k in ks:
            copies.append(pltpu.make_async_copy(near[k], far[k], sems.at[k]))
            copies[-1].start()

    late = sum(part[3 * n :, :].astype(F32) for part in parts)
    scale = vec[1:2, :]
    diag = lax.broadcasted_iota(jnp.int32, (n, n), 0) == lax.broadcasted_iota(jnp.int32, (n, n), 1)

    def column(row):
        return jnp.sum(jnp.where(diag, jnp.broadcast_to(row, (n, n)), 0.0), axis=1, keepdims=True)

    def row(col):
        return jnp.sum(jnp.where(diag, jnp.broadcast_to(col, (n, n)), 0.0), axis=0, keepdims=True)

    def take(start, size):
        return small[:, start : start + size] + small[:, start + size : start + 2 * size]

    m = late[:n]
    cols = (late[n : n + 1] + late[n + 1 : n + 2]) * scale
    small = late[n + 2 : n + 3]
    m_scaled = m * scale
    weight = proj[...].astype(F32)
    gains, shifts, skips = (a[...].astype(F32) for a in (gain, shift, skip))
    in_out[...] = column(gains) * m_scaled + column(shifts) * cols
    ready(2)
    s1, s2 = take(SIDE, n), take(SIDE + 2 * n, n)
    gain_out[...] = row(jnp.sum(m_scaled * weight, axis=1, keepdims=True)) + skips * s1
    shift_out[...] = row(jnp.sum(cols * weight, axis=1, keepdims=True)) + skips * s2
    skip_out[...] = gains * s1 + shifts * s2
    bias_out[...] = 0.5 * take(SIDE + 4 * n, 2 * n)
    re, im = take(0, q), take(2 * q, q)
    gamma_out[...] = take(4 * q, q)
    rate = jnp.exp(decay[...].astype(F32))
    turn = jnp.exp(phase[...].astype(F32))
    modulus = jnp.exp(-rate)
    lam_re, lam_im = modulus * jnp.cos(turn), modulus * jnp.sin(turn)
    decay_out[...] = -rate * (re * lam_re + im * lam_im)
    phase_out[...] = turn * (im * lam_re - re * lam_im)
    ready(3, 4, 5, 6, 7, 8, 9)
    early = sum(part[: 3 * n, :].astype(F32) for part in parts)
    gate_out[:, :width] = 0.5 * early[:n]
    gate_out[:, width:] = 0.5 * early[n : 2 * n]
    proj_out[...] = early[2 * n :]
    ready(0, 1)
    for copy in copies:
        copy.wait()


def swap(a, axis, size, bit):
    return lax.ppermute(a, axis, [(k, k ^ bit) for k in range(size)])


def spread(a, axis, size):
    return jnp.stack([a] + [swap(a, axis, size, k) for k in range(1, size)])


def cross_pairs(owners, tmc, turn):
    return [(k, k ^ (2 * tmc << (k % 2 ^ turn))) for k in range(owners)]


def tie(first, *rest):
    return lax.optimization_barrier((first, *rest))


def cmul_rows(row, a):
    half = a.shape[1] // 2
    re, im = complex_mul(row[:half], row[half:], a[:, :half], a[:, half:])
    return jnp.concatenate([re, im], axis=1)


def carry_in(end, pows, bits, sizes, backward, during):
    total, pre = end, jnp.zeros_like(end)
    for bit in range(bits):
        total = during(bit, total)
        if bit == 0:
            got = swap(total, "core", 2, 1)
        else:
            got = swap(total, "tmc", sizes["tmc"], 1 << (bit - 1))
        taken = pows[4 * bits + bit][None]
        later = taken < 0.5 if backward else taken > 0.5
        wide = pows[4 * bit + (3 if backward else 0)]
        pre = pre + cmul_rows(pows[4 * bit + (2 if backward else 1)], got)
        total = jnp.where(later, total, got) + cmul_rows(wide, jnp.where(later, got, total))
    return pre


def add_low(*parts):
    return sum(a.astype(F32) for a in parts).astype(BF)


def make_body(sizes):
    chips = sizes["seq"] * sizes["tmc"]
    owners = chips * 2
    bits = (2 * sizes["tmc"]).bit_length() - 1

    def body(
        tokens, lengths, cotangent, norm_gain, norm_shift, input_proj, decay_log, phase_log,
        gamma_log, output_proj, skip_gain, gate_weight, gate_bias,
    ):
        micro, per, length, width = tokens.shape
        count = micro * per
        total = count * length
        half = width // 2
        n = width // owners
        fast = n % 16 == 0 and sizes["seq"] == 4
        tok = tokens.reshape(count, length, width)
        cot = cotangent.reshape(count, length, width)
        wide_bf, wide_f = ((total, width), BF), ((total, width), F32)

        vectors = (norm_gain, norm_shift, skip_gain, decay_log, phase_log, gamma_log, gate_bias)
        lead = n + 8
        ins = [v.reshape(1, -1) for v in vectors] + [input_proj, output_proj, gate_weight]
        pack, flag = call(
            pack_kernel, "pack", [((4 * n + 8, width), BF), ((1, width), F32)], ins, [(a.shape, BF) for a in ins],
            far_in=range(10) if fast else (), copies=10,
        )

        def whiten(t):
            thin = ((total, SIDE), F32)
            return call(
                whiten_kernel, "whiten", [wide_bf, thin], (t,), [thin], far_out=(1,), copies=length // 64
            )

        def mask(ct):
            return call(mask_kernel, "mask", [wide_f], (lengths.T, ct))[0]

        powers = ((-(-5 * bits // 8) * 8, width), F32)
        if fast:
            along = spread(pack, "tmc", sizes["tmc"])
            wh, inv = whiten(tok)
            along, wh = tie(along, wh)
            own_first = spread(along[:, :lead], "seq", sizes["seq"]).reshape(chips, lead, width)
            rest = along[:, lead:]
            rest = [rest] + [swap(rest, "seq", sizes["seq"], k) for k in (1, 2)]
            own_first, *rest = tie(own_first, *rest)
            other_first = swap(own_first, "core", 2, 1)
            forward = jnp.where(flag > 0.5, rest[2], rest[1])
            rest.append(lax.ppermute(forward, AXES, cross_pairs(owners, sizes["tmc"], 1)))
            b, vec, pows, u, end = call(
                lambda *r: drive_gathered_kernel(bits, *r), "drive",
                [((width, width), BF), ((8, width), F32), powers, wide_f, ((count, width), F32)],
                (own_first, other_first, wh),
            )
        else:
            wh, inv = whiten(tok)
            cotl = mask(cot)
            every = lax.all_gather(pack, AXES)
            vec = jnp.sum(every[:, n:lead].astype(F32), axis=0)
            vec = jnp.concatenate(vector_rows(vec), axis=0)
            mats = [every[:, :n]] + [every[:, lead + k * n : lead + (k + 1) * n] for k in range(3)]
            mats = [a.reshape(width, width) for a in mats]
            b = (mats[0].astype(F32) * vec[1:2]).astype(BF)
            c = mats[1]
            g = (jnp.concatenate(mats[2:], axis=1).astype(F32) * 0.5).astype(BF)
            pows, u, end = call(
                lambda *r: drive_plain_kernel(bits, *r), "drive",
                [powers, wide_f, ((count, width), F32)], (b, vec, wh),
            )

        held = {}

        def early_rest(bit, a):
            if fast and bit == 1:
                a, rest[3], late_cot = tie(a, rest[3], cot)
                held["cotl"] = mask(late_cot)
            if fast and bit == 2:
                a, held["cotl"] = tie(a, held["cotl"])
                parts = tie(a, *rest)[1:]
                held["own"] = jnp.stack(parts).reshape(chips, -1, width)
                held["other"] = swap(held["own"], "core", 2, 1)
            return a

        carry = carry_in(end, pows, bits, sizes, False, early_rest)
        if fast:
            cotl = held["cotl"]
        rows = 256
        blocks = total // rows
        side = ((count, length, width), BF)
        outs = [
            wide_bf, wide_f, wide_bf, ((total, 2 * width), BF), wide_bf, wide_bf,
            ((count, width), F32), ((4, width), F32),
        ]
        scratch = [
            ((2, rows, width), F32), ((2, rows, 2 * width), F32), ((4, rows, width), F32),
            ((2, rows, width), F32),
        ]
        if fast:
            ins = (u, cotl, carry, vec, held["own"], held["other"], wh)
            scratch += [((width, width), BF), ((width, 2 * width), BF)]
        else:
            ins = (u, cotl, carry, vec, c, g, wh)
        st, dst, act, dpre, dm, y, back_end, sums = call(
            middle_gathered_kernel if fast else middle_body, "middle", outs, ins, scratch,
            limit=24,
        )
        if not fast:
            (out_grads,) = call(
                weights_plain_kernel, "weights", [((width, 3 * width), BF)], (act, dpre, st, dm)
            )

        def seq_parts(both):
            both = both.reshape(sizes["seq"], sizes["tmc"], -1, width)
            return [both[0]] + [swap(both[k], "seq", sizes["seq"], k) for k in range(1, sizes["seq"])]

        def early_sums(bit, a):
            if fast and bit == 1:
                now = tie(a, act)[1]
                held["sums"] = call(
                    weights_gathered_kernel, "weights", [((chips, 48, width), BF)] * 2,
                    (now, dpre, st, dm), [((3, width, width), BF)],
                )
            if fast and bit == 2:
                a, *held["sums"] = tie(a, *held["sums"])
                held["got"] = swap(held["sums"][1], "core", 2, 1)
            return a

        back = carry_in(back_end, pows, bits, sizes, True, early_sums)
        if fast:
            got = held["got"]
            low, high = (
                add_low(held["sums"][0][k : k + chips // 2], got[k : k + chips // 2])
                for k in (0, chips // 2)
            )
            quarter = chips // 4
            first_link = cross_pairs(owners, sizes["tmc"], 0)
            got = [lax.ppermute(high[k : k + quarter], AXES, first_link) for k in (quarter, 0)]
            held["early"] = (low, *got)

        ins = (dst, u, st, wh, back, carry, vec)
        if fast:
            adj, late_keep, late_give = call(
                adjoint_gathered_kernel, "adjoint",
                [wide_bf] + [((chips, 24, width), BF)] * 2, (*ins, sums),
                [((width, width), BF), ((owners, 2 * SIDE), F32)], limit=10,
            )
            low, got, got_own = held["early"]
            give = add_low(low[quarter:], got)
            give, late_keep, late_give = tie(give, late_keep, late_give)
            got = lax.ppermute(give, AXES, cross_pairs(owners, sizes["tmc"], 1))
            late = add_low(late_keep, swap(late_give, "core", 2, 1))
            late, y = tie(late, y)
            early = add_low(low[:quarter], got_own, got)
            both = jnp.concatenate([early, add_low(*seq_parts(late))], axis=1)
            block_out = call(
                output_kernel, "output", [side], (lengths.T, y, tok), [side],
                limit=6, far_out=(0,), copies=4,
            )[0]
            both, adj, block_out = tie(both, adj, block_out)
            both = [both[0]] + [swap(both[k], "tmc", sizes["tmc"], k) for k in range(1, sizes["tmc"])]
        else:
            adj, m, late_rows = call(
                adjoint_plain_kernel, "adjoint",
                [wide_bf, ((width, width), BF), ((8, width), F32)], ins, limit=10,
            )
            block_out = call(
                output_kernel, "output", [side], (lengths.T, y, tok), [side],
                limit=6, far_out=(0,), copies=4,
            )[0]
        (tok_grad,) = call(
            inputs_kernel, "inputs", [side], (adj, dm, cot, inv, wh, b, vec),
            [side, ((2, rows, width), F32)], limit=8, far_out=(0,), copies=blocks,
        )

        q = half // owners
        if fast:
            shapes = [(n, 2 * width), (n, width), (n, width)] + [(1, n)] * 3 + [(1, q)] * 3 + [(1, 2 * n)]
            shapes = [(a, F32) for a in shapes]
            rows = [v.reshape(1, -1) for v in (norm_gain, norm_shift, skip_gain, decay_log, phase_log)]
            grads = call(
                finish_kernel, "finish", shapes, (vec, input_proj, *rows, *both), shapes,
                far_out=range(10), copies=10,
            )
            gate_sum, proj_sum, in_grad = grads[:3]
            gain_grad, shift_grad, skip_grad, decay_grad, phase_grad, gamma_grad, bias_sum = (
                a.reshape(-1) for a in grads[3:]
            )
        else:
            def scatter(a):
                return lax.psum_scatter(a.astype(F32), AXES, scatter_dimension=0, tiled=True)

            gate_sum = scatter(out_grads[:, : 2 * width]) * 0.5
            proj_sum = scatter(out_grads[:, 2 * width :])
            m_sum = scatter(m)
            cols = lax.psum(late_rows[0], AXES)
            lam_re_sum = scatter(late_rows[1, :half])
            lam_im_sum = scatter(late_rows[1, half:])
            gamma_grad = scatter(late_rows[2, :half])
            s1, s2 = scatter(sums[0]), scatter(sums[1])
            bias_sum = scatter(sums[2:].reshape(2 * width)) * 0.5
            gain = norm_gain.astype(F32)
            shift = norm_shift.astype(F32)
            skip = skip_gain.astype(F32)
            proj = input_proj.astype(F32)
            scale = vec[1]
            in_grad = (gain[:, None] * m_sum + shift[:, None] * cols[None]) * scale[None]
            gain_grad = jnp.sum(m_sum * scale[None] * proj, axis=1) + skip * s1
            shift_grad = jnp.sum((cols * scale)[None] * proj, axis=1) + skip * s2
            skip_grad = gain * s1 + shift * s2
            rate = jnp.exp(decay_log.astype(F32))
            phase = jnp.exp(phase_log.astype(F32))
            modulus = jnp.exp(-rate)
            lam_re = modulus * jnp.cos(phase)
            lam_im = modulus * jnp.sin(phase)
            decay_grad = -rate * (lam_re_sum * lam_re + lam_im_sum * lam_im)
            phase_grad = phase * (lam_im_sum * lam_re - lam_re_sum * lam_im)
        return (
            block_out.reshape(tokens.shape), tok_grad.reshape(tokens.shape), gain_grad, shift_grad,
            in_grad, decay_grad, phase_grad, gamma_grad, proj_sum, skip_grad, gate_sum, bias_sum,
        )

    return body


def solution(mesh):
    seq, tm = mesh.shape["seq"], mesh.shape["tm"]
    fine = Mesh(mesh.devices.reshape(seq, tm // 2, 2), AXES)
    sizes = dict(zip(AXES, (seq, tm // 2, 2)))
    side = P(None, "seq", ("tmc", "core"), None)
    vec = P(AXES)
    mat = P(AXES, None)
    return jax.shard_map(
        make_body(sizes),
        mesh=fine,
        in_specs=(side, P(None, "seq"), side, vec, vec, mat, vec, vec, vec, mat, vec, mat, vec),
        out_specs=(side, side, vec, vec, mat, vec, vec, vec, mat, vec, mat, vec),
        check_vma=False,
    )
```
